512 devices in a mesh: lat: 8 (over x, core), lon: 16 (over z_hi, y), fsdp: 4 (over z_lo).
Axes of the slice: x: 4, y: 8, z: 8 (z_hi: 2, z_lo: 4; z = z_hi * 4 + z_lo), core: 2. Of those that a mesh axis runs over, the one named last changes fastest.
Arguments:
- tokens: bfloat16 [64, 256, 1024], P('lat', 'lon'), may hold values from -8 to 8
- grad_out: bfloat16 [64, 256, 1024], P('lat', 'lon', 'fsdp'), may hold values from -6 to 6
- weight: bfloat16 [3, 1024, 1024], P(None, 'fsdp'), may hold values from -4 to 4
Outputs:
- grad_input: bfloat16 [64, 256, 1024], P('lat', 'lon', 'fsdp')
- grad_weight: float32 [3, 1024, 1024], P(None, ('lat', 'lon'), 'fsdp')
The draws below stay inside these ranges and needn't reach their ends.
All inputs are finite; a program needn't handle non-finite values.
Results may differ from the reference program's by a relative error of at most 0.011.
The reference program's roundings to bfloat16 on the way (of `grad_score` and `prob_rounded`) count: a program that leaves them out, or rounds other values in their place, can miss the bound.
Values may be sent and summed in bfloat16 or wider, within the bound.
A program may use at most 64 MiB of HBM per device.

```python
import math
import jax
import jax.numpy as jnp
from jax import lax

D = 1024
HEADS = 16
RADIUS = 6
CO = 16
NLAT = 64
NLON = 256
TOKENS = 16384


def draw_tokens(key, part):
    values = jnp.clip(jax.random.normal(key, (NLAT, NLON, D), jnp.float32), -6.0, 6.0)
    return values.astype(jnp.bfloat16)


def draw_weight(key, part):
    k_normal = jax.random.fold_in(key, 0)
    spread = D ** (-0.5)
    normal_part = jnp.clip(jax.random.normal(k_normal, (3, D, D), jnp.float32), -6.0, 6.0) * spread
    return jnp.clip(normal_part, -4.0, 4.0).astype(jnp.bfloat16)


def steps_of(stream_key, extent, shards, low, high):
    def one(position, parts):
        heights = jax.random.uniform(jax.random.fold_in(jax.random.fold_in(stream_key, 6), position), (parts,), jnp.float32, low / len(shards), high / len(shards))
        return jnp.repeat(jnp.exp(heights), extent[position] // parts).reshape((-1,) + (1,) * (len(extent) - position - 1))

    factor_of = one(*shards[0])
    for cut in shards[1:]:
        factor_of = factor_of * one(*cut)
    return factor_of


def noise(own_key, extent, width, limit, cuts=(), held_as=jnp.bfloat16):
    loudness = steps_of(own_key, extent, cuts, -0.22, 0.18) if cuts else 1.0
    array = jax.random.normal(own_key, extent, jnp.float32) * width * loudness
    return jnp.minimum(jnp.maximum(array, -limit), limit).astype(held_as)


def setup_inputs(seed: int = 0) -> dict:
    key_of = jax.random.split(jax.random.key(seed), 4)
    tokens = draw_tokens(jax.random.fold_in(key_of[3], 71), 0)
    grad_out = noise(key_of[1], (NLAT, NLON, D), 1.0, 6.0, ((0, 8), (1, 16), (2, 4)))
    weight = draw_weight(jax.random.fold_in(key_of[3], 71), 0)
    return {"tokens": tokens, "grad_out": grad_out, "weight": weight}


def fold_band(band_terms, row_count):
    band_width = band_terms.shape[0]
    padding_rest = ((0, 0),) * (band_terms.ndim - 2)
    running = jnp.zeros((row_count + band_width - 1,) + band_terms.shape[2:], jnp.float32)
    for offset in range(band_width):
        running = running + jnp.pad(band_terms[offset], ((offset, band_width - 1 - offset),) + padding_rest)
    return running

def reference(tokens, grad_out, weight):
    head_size = D // HEADS
    score_scale = 1.0 / math.sqrt(head_size)
    window_reach = 2 * RADIUS + 1
    col_blocks = NLON // CO
    ext_cols = CO + 2 * RADIUS
    flat_tokens = tokens.reshape(TOKENS, D)
    projected = [jnp.dot(flat_tokens, weight[number], preferred_element_type=jnp.float32).astype(jnp.bfloat16).reshape(NLAT, NLON, D) for number in range(3)]
    queries_all, keys_all, values_all = projected
    row_index = jnp.arange(window_reach)[:, None] + jnp.arange(NLAT)[None, :] - RADIUS
    lat_ok = (row_index >= 0) & (row_index < NLAT)
    col_gap = jnp.arange(ext_cols)[None, :] - jnp.arange(CO)[:, None] - RADIUS
    lon_ok = jnp.abs(col_gap) <= RADIUS
    allowed = lat_ok[:, :, None, None] & lon_ok[None, None]

    def widen(field_head):
        wrapped = jnp.concatenate([field_head[:, NLON - RADIUS:], field_head, field_head[:, :RADIUS]], 1)
        return jnp.pad(wrapped, ((RADIUS, RADIUS), (0, 0), (0, 0)))

    def split_cols(field_head, band_width):
        return jnp.stack([field_head[:, block * CO:block * CO + band_width] for block in range(col_blocks)])

    def one_block(block_items):
        query_block, key_block, value_block, grad_block = block_items
        key_band = jnp.stack([key_block[offset:offset + NLAT] for offset in range(window_reach)])
        value_band = jnp.stack([value_block[offset:offset + NLAT] for offset in range(window_reach)])
        scores = score_scale * jnp.einsum('rqd,arkd->arqk', query_block, key_band)
        scores = jnp.where(allowed, scores, -jnp.inf)
        row_max = lax.optimization_barrier(jnp.max(scores, axis=(0, 3), keepdims=True))
        exp_scores = jnp.exp(scores - row_max)
        attn_prob = exp_scores / lax.optimization_barrier(jnp.sum(exp_scores, axis=(0, 3), keepdims=True))
        grad_prob = jnp.einsum('rqd,arkd->arqk', grad_block, value_band)
        delta_row = lax.optimization_barrier(jnp.sum(attn_prob * grad_prob, axis=(0, 3), keepdims=True))
        grad_score = lax.optimization_barrier((score_scale * (attn_prob * (grad_prob - delta_row))).astype(jnp.bfloat16)).astype(jnp.float32)
        prob_rounded = lax.optimization_barrier(attn_prob.astype(jnp.bfloat16)).astype(jnp.float32)
        query_grad = jnp.einsum('arqk,arkd->rqd', grad_score, key_band)
        key_grad = fold_band(jnp.einsum('arqk,rqd->arkd', grad_score, query_block), NLAT)
        value_grad = fold_band(jnp.einsum('arqk,rqd->arkd', prob_rounded, grad_block), NLAT)
        return (query_grad, key_grad, value_grad)

    def gather_back(ext_blocks):
        running = jnp.zeros((NLAT + 2 * RADIUS, NLON + 2 * RADIUS, head_size), jnp.float32)
        for block in range(col_blocks):
            running = running.at[:, block * CO:block * CO + ext_cols].add(ext_blocks[block])
        inner_rows = running[RADIUS:RADIUS + NLAT]
        centre_part = inner_rows[:, RADIUS:RADIUS + NLON]
        centre_part = centre_part.at[:, NLON - RADIUS:].add(inner_rows[:, :RADIUS])
        centre_part = centre_part.at[:, :RADIUS].add(inner_rows[:, NLON + RADIUS:])
        return centre_part

    def one_head(head_number):
        first_col = head_number * head_size

        def pick_head(field_all):
            return lax.dynamic_slice_in_dim(field_all, first_col, head_size, 2).astype(jnp.float32)
        query_head = pick_head(queries_all)
        key_head = pick_head(keys_all)
        value_head = pick_head(values_all)
        grad_head = pick_head(grad_out)
        block_items = (split_cols(query_head, CO), split_cols(widen(key_head), ext_cols), split_cols(widen(value_head), ext_cols), split_cols(grad_head, CO))
        query_blocks, key_blocks, value_blocks = lax.map(one_block, block_items)
        query_grad = jnp.concatenate([query_blocks[block] for block in range(col_blocks)], 1)
        return (query_grad.astype(jnp.bfloat16), gather_back(key_blocks).astype(jnp.bfloat16), gather_back(value_blocks).astype(jnp.bfloat16))
    head_grads = lax.map(one_head, jnp.arange(HEADS, dtype=jnp.int32))
    grad_rows = [jnp.transpose(stacked, (1, 2, 0, 3)).reshape(TOKENS, D) for stacked in head_grads]
    input_sum = jnp.dot(grad_rows[0], weight[0].T, preferred_element_type=jnp.float32)
    input_sum = input_sum + jnp.dot(grad_rows[1], weight[1].T, preferred_element_type=jnp.float32)
    input_sum = input_sum + jnp.dot(grad_rows[2], weight[2].T, preferred_element_type=jnp.float32)
    grad_input = input_sum.astype(jnp.bfloat16).reshape(NLAT, NLON, D)
    weight_scale = 1.0 / math.sqrt(TOKENS)
    grad_weight = jnp.stack([jnp.dot(flat_tokens.T, grad_rows[number], preferred_element_type=jnp.float32) * weight_scale for number in range(3)])
    return (grad_input, grad_weight)
```

```python
import functools
import math

import jax
import jax.numpy as jnp
from jax import lax
from jax.experimental import pallas as pl
from jax.experimental.pallas import tpu as pltpu
from jax.sharding import PartitionSpec as P

HEADS = 16
RADIUS = 6
MESH = pl.DeviceIdType.MESH
BF16 = jnp.bfloat16
F32 = jnp.float32

ROWS, COLS = 8, 16
TOK = ROWS * COLS
BLOCKS = 6
EXT = BLOCKS * TOK
SLAB = RADIUS * ROWS
EAST, WEST = 0, 64
LATS, LONS, FSDP = 8, 16, 4
XS, YS, ZS = 4, 8, 8

NORTH_SOUTH, EAST_WEST, CORNERS = 0, 2, 4
GRADS = 8
WEIGHTS, CORE_WEIGHTS = 16, 19
STATS = 22
CORE_GRAD = 30
INPUT_SUMS = 31
SUM_X, SUM_Y, SUM_Z = 34, 37, 44
COPIES = 45


def dot(a, b, ca, cb, precision=None):
    return lax.dot_general(
        a, b, (((ca,), (cb,)), ((), ())), preferred_element_type=F32, precision=precision
    )


def place(block, spot):
    half = spot // 64
    inner = spot % 64
    side_col = inner // ROWS + jnp.where(half == 0, COLS, -RADIUS)
    is_tile = block < 3
    row = jnp.where(is_tile, spot // COLS, inner % ROWS)
    col = jnp.where(is_tile, spot % COLS, side_col)
    kind = block % 3
    shift = jnp.where(kind == 1, -ROWS, jnp.where(kind == 2, ROWS, 0))
    real = is_tile | (inner < SLAB)
    return row + shift, col, real


def bias_of(block, spot, own, lat):
    row, col, real = place(block, spot)
    own_row, own_col = own // COLS, own % COLS
    gap_r = row - own_row
    gap_c = col - own_col
    grid_row = lat * ROWS + row
    allowed = (
        real
        & (gap_r <= RADIUS)
        & (gap_r >= -RADIUS)
        & (gap_c <= RADIUS)
        & (gap_c >= -RADIUS)
        & (grid_row >= 0)
        & (grid_row < LATS * ROWS)
    )
    return jnp.where(allowed, 0.0, -jnp.inf).astype(F32)


def kernel(
    tokens,
    grad_out,
    weight,
    grad_input,
    grad_weight,
    xs,
    dos,
    packs,
    wbuf,
    qkv,
    bias_f,
    bias_b,
    stats,
    stats_in,
    stat_rows,
    grads,
    x2,
    acc,
    gi_own,
    gi_out,
    gi_in,
    gx_out,
    gx_in,
    r1,
    gy_out,
    gy_in,
    r2,
    gz_in,
    send_sems,
    recv_sems,
    local_sems,
):
    lat = lax.axis_index("lat")
    lon = lax.axis_index("lon")
    fsdp = lax.axis_index("fsdp")
    x, core = lat // 2, lat % 2
    z_hi, y = lon // YS, lon % YS
    z = z_hi * FSDP + fsdp
    head_size = 64
    own_heads = HEADS // FSDP
    own_cols = own_heads * head_size
    width = FSDP * own_cols
    scale = 1.0 / math.sqrt(head_size)

    def at(*, d_lat=None, d_lon=None, d_fsdp=None):
        return (
            lat if d_lat is None else d_lat,
            lon if d_lon is None else d_lon,
            fsdp if d_fsdp is None else d_fsdp,
        )

    south_lat, north_lat = (lat + 1) % LATS, (lat + LATS - 1) % LATS
    east_lon, west_lon = (lon + 1) % LONS, (lon + LONS - 1) % LONS
    east_fsdp = jnp.where(y == YS - 1, FSDP - 1 - fsdp, fsdp)
    west_fsdp = jnp.where(y == 0, FSDP - 1 - fsdp, fsdp)
    south, north = at(d_lat=south_lat), at(d_lat=north_lat)
    east, west = at(d_lon=east_lon), at(d_lon=west_lon)
    east_copy = at(d_lon=east_lon, d_fsdp=east_fsdp)
    west_copy = at(d_lon=west_lon, d_fsdp=west_fsdp)
    other_core = at(d_lat=lat + 1 - 2 * core)

    def on_z(step):
        target = (z + step + ZS) % ZS
        return at(d_lon=(target // FSDP) * YS + y, d_fsdp=target % FSDP)

    def on_x(step):
        return at(d_lat=((x + step) % XS) * 2 + core)

    def on_y(step):
        return at(d_lon=z_hi * YS + (y + step) % YS)

    z_partner = at(d_lon=(1 - z_hi) * YS + y)
    corners = (
        at(d_lat=north_lat, d_lon=east_lon),
        at(d_lat=north_lat, d_lon=west_lon),
        at(d_lat=south_lat, d_lon=east_lon),
        at(d_lat=south_lat, d_lon=west_lon),
    )
    partners = [south, north, east, west, east_copy, west_copy, *corners]
    partners += [on_z(step) for step in (1, -1, 2, -2)]
    partners += [at(d_fsdp=(fsdp + step) % FSDP) for step in range(1, FSDP)]
    partners += [on_x(step) for step in range(1, XS)]
    partners += [on_y(step) for step in range(1, YS)]
    partners += [z_partner]

    barrier = pltpu.get_barrier_semaphore()
    for partner in partners:
        pl.semaphore_signal(barrier, inc=1, device_id=partner, device_id_type=MESH)

    own_tokens = pltpu.make_async_copy(tokens, xs.at[pl.ds(0, TOK)], local_sems.at[0])
    own_grads = pltpu.make_async_copy(grad_out, dos.at[pl.ds(0, TOK)], local_sems.at[1])
    own_start = pl.multiple_of(fsdp * own_cols, own_cols)
    own_weight = pltpu.make_async_copy(
        weight.at[:, :, pl.ds(own_start, own_cols)],
        wbuf.at[:, pl.ds(own_start, own_cols), :],
        local_sems.at[2],
    )
    own_tokens.start()
    own_grads.start()
    own_weight.start()

    def remote(src, dst, number, device):
        return pltpu.make_async_remote_copy(
            src_ref=src,
            dst_ref=dst,
            send_sem=send_sems.at[number],
            recv_sem=recv_sems.at[number],
            device_id=device,
            device_id_type=MESH,
        )

    pl.semaphore_wait(barrier, len(partners))

    sent = []

    def start(*args):
        copy = remote(*args)
        copy.start()
        sent.append(copy)
        return copy

    half_rows = own_cols // 2
    far = 2 - 4 * core
    weight_copies = []
    for number, step in enumerate((1, -1, far)):
        target = on_z(step)
        cols = pl.multiple_of(target[2] * own_cols, own_cols)
        rows = pl.multiple_of(fsdp * own_cols + core * half_rows, half_rows)
        weight_copies.append(
            start(
                weight.at[:, pl.ds(core * half_rows, half_rows), pl.ds(cols, own_cols)],
                wbuf.at[:, pl.ds(rows, half_rows), :],
                WEIGHTS + number,
                target,
            )
        )

    own_tokens.wait()
    own_grads.wait()
    tile_copies = []
    for number, device, block in ((0, south, 1), (1, north, 2)):
        tile_copies.append(
            start(
                xs.at[pl.ds(0, TOK)], xs.at[pl.ds(block * TOK, TOK)], NORTH_SOUTH + number, device
            )
        )
    spot = lax.broadcasted_iota(jnp.int32, (TOK, TOK), 0)
    flat = lax.broadcasted_iota(jnp.int32, (TOK, TOK), 1)
    inner = spot % 64
    source = (inner % ROWS) * COLS + inner // ROWS + jnp.where(spot < 64, 0, COLS - RADIUS)
    picks = (inner < SLAB) & (flat == source)
    pick = jnp.where(picks, 1.0, 0.0).astype(F32)
    pick_16 = pick.astype(BF16)
    packs[:, pl.ds(0, width)] = dot(pick_16, xs[pl.ds(0, TOK), :], 1, 0).astype(BF16)
    packs[:, pl.ds(width, own_cols)] = dot(pick_16, dos[pl.ds(0, TOK), :], 1, 0).astype(BF16)
    side_copies = []
    side = 3 * TOK
    for number, spot_at, token_device in ((0, EAST, west_copy), (1, WEST, east_copy)):
        side_copies.append(
            start(
                packs.at[pl.ds(spot_at, SLAB), pl.ds(0, width)],
                xs.at[pl.ds(side + spot_at, SLAB)],
                EAST_WEST + number,
                token_device,
            )
        )
    grad_tile_copies = []
    grad_side_copies = []
    for number, spot_at, device in ((0, EAST, west), (1, WEST, east)):
        grad_side_copies.append(
            start(
                packs.at[pl.ds(spot_at, SLAB), pl.ds(width, own_cols)],
                dos.at[pl.ds(side + spot_at, SLAB)],
                GRADS + EAST_WEST + number,
                device,
            )
        )
    for number, device, block in ((0, south, 1), (1, north, 2)):
        grad_tile_copies.append(
            start(
                dos.at[pl.ds(0, TOK)],
                dos.at[pl.ds(block * TOK, TOK)],
                GRADS + NORTH_SOUTH + number,
                device,
            )
        )

    for block in range(3, BLOCKS):
        for spot_at in (EAST, WEST):
            unused = pl.ds(block * TOK + spot_at + SLAB, 64 - SLAB)
            xs[unused, :] = jnp.zeros((64 - SLAB, width), BF16)
            dos[unused, :] = jnp.zeros((64 - SLAB, own_cols), BF16)

    @pl.loop(0, BLOCKS)
    def _(block):
        first = pl.multiple_of(block * TOK, TOK)
        bias_f[pl.ds(first, TOK), :] = bias_of(block, spot, flat, lat)
        bias_b[:, pl.ds(first, TOK)] = bias_of(block, flat, spot, lat)

    corner_copies = []
    for number, spot_at in ((0, EAST), (1, WEST)):
        side_copies[number].wait_recv()
        for leg, (device, block) in enumerate(((south, 4), (north, 5))):
            corner_copies.append(
                start(
                    xs.at[pl.ds(side + spot_at, SLAB)],
                    xs.at[pl.ds(block * TOK + spot_at, SLAB)],
                    CORNERS + 2 * number + leg,
                    device,
                )
            )
    core_weight_copies = []
    for number, step in enumerate((-1, 1, -far)):
        weight_copies[number].wait_recv()
        origin = (fsdp + step + FSDP) % FSDP
        rows = pl.multiple_of(origin * own_cols + core * half_rows, half_rows)
        region = wbuf.at[:, pl.ds(rows, half_rows), :]
        core_weight_copies.append(start(region, region, CORE_WEIGHTS + number, other_core))
    for number, spot_at in ((0, EAST), (1, WEST)):
        grad_side_copies[number].wait_recv()
        for leg, (device, block) in enumerate(((south, 4), (north, 5))):
            corner_copies.append(
                start(
                    dos.at[pl.ds(side + spot_at, SLAB)],
                    dos.at[pl.ds(block * TOK + spot_at, SLAB)],
                    GRADS + CORNERS + 2 * number + leg,
                    device,
                )
            )

    own_weight.wait()
    for copy in tile_copies + core_weight_copies + corner_copies[:4]:
        copy.wait_recv()

    @pl.loop(0, EXT // 256)
    def _(step):
        rows = pl.ds(pl.multiple_of(step * 256, 256), 256)
        block = xs[rows, :]
        for number in range(3):
            qkv[number, rows, :] = dot(block, wbuf[number], 1, 0).astype(BF16)

    lane = lax.broadcasted_iota(jnp.int32, (TOK, own_cols), 1) // head_size
    own = pl.ds(0, TOK)

    stats[pl.ds(3 * own_heads, own_heads), :] = jnp.zeros((own_heads, TOK), F32)

    @pl.loop(0, own_heads)
    def _(head):
        mine = lane == head
        query = jnp.where(mine, qkv[0, own, :], 0).astype(BF16)
        cotangent = jnp.where(mine, dos[own, :], 0).astype(BF16)
        scores = dot(qkv[1], query, 1, 1) * scale + bias_f[...]
        row_max = jnp.max(scores, axis=0, keepdims=True)
        prob = jnp.exp(scores - row_max)
        inv_sum = 1.0 / jnp.sum(prob, axis=0, keepdims=True)
        prob = prob * inv_sum
        grad_prob = dot(qkv[2], cotangent, 1, 1)
        delta = jnp.sum(prob * grad_prob, axis=0, keepdims=True)
        grad_score = (scale * (prob * (grad_prob - delta))).astype(BF16)
        part = dot(grad_score, qkv[1], 0, 0)
        acc[0] = jnp.where(mine, part, acc[0])
        stats[pl.ds(head, 1), :] = row_max
        stats[pl.ds(own_heads + head, 1), :] = inv_sum
        stats[pl.ds(2 * own_heads + head, 1), :] = delta

    stats[pl.ds(16, 16), :] = dot(
        stats[pl.ds(0, 16), :], pick, 1, 1, precision=lax.Precision.HIGHEST
    )
    tile_stats = stats.at[pl.ds(0, 16)]
    side_stats = stats.at[pl.ds(16, 16)]
    stat_copies = []
    for number, (src, device) in enumerate(
        (
            (tile_stats, south),
            (tile_stats, north),
            (side_stats, west),
            (side_stats, east),
            (side_stats, corners[3]),
            (side_stats, corners[2]),
            (side_stats, corners[1]),
            (side_stats, corners[0]),
        )
    ):
        stat_copies.append(start(src, stats_in.at[number], STATS + number, device))
    for copy in grad_tile_copies + corner_copies[4:] + stat_copies:
        copy.wait_recv()
    half_lane = lax.broadcasted_iota(jnp.int32, (16, TOK), 1) < 64
    stat_rows[:, pl.ds(0, TOK)] = stats[pl.ds(0, 16), :]
    stat_rows[:, pl.ds(TOK, TOK)] = stats_in[0]
    stat_rows[:, pl.ds(2 * TOK, TOK)] = stats_in[1]
    for block in range(3):
        first = 2 + 2 * block
        stat_rows[:, pl.ds((3 + block) * TOK, TOK)] = jnp.where(
            half_lane, stats_in[first], stats_in[first + 1]
        )

    @pl.loop(0, own_heads)
    def _(head):
        mine = lane == head
        key = jnp.where(mine, qkv[1, own, :], 0).astype(BF16)
        value = jnp.where(mine, qkv[2, own, :], 0).astype(BF16)
        row_max = stat_rows[pl.ds(head, 1), :]
        inv_sum = stat_rows[pl.ds(own_heads + head, 1), :]
        delta = stat_rows[pl.ds(2 * own_heads + head, 1), :]
        scores = dot(key, qkv[0], 1, 1) * scale + bias_b[...]
        prob = jnp.exp(jnp.minimum(scores - row_max, 0.0)) * inv_sum
        grad_prob = dot(value, dos[...], 1, 1)
        grad_score = (scale * (prob * (grad_prob - delta))).astype(BF16)
        acc[1] = jnp.where(mine, dot(grad_score, qkv[0], 1, 0), acc[1])
        acc[2] = jnp.where(mine, dot(prob.astype(BF16), dos[...], 1, 0), acc[2])

    for number in range(3):
        grads[own, pl.ds(number * own_cols, own_cols)] = acc[number].astype(BF16)

    core_grad = start(grads.at[own], grads.at[pl.ds(TOK, TOK)], CORE_GRAD, other_core)

    def input_terms(owner):
        rows = pl.ds(pl.multiple_of(owner * own_cols, own_cols), own_cols)
        total = None
        for number in range(3):
            term = dot(
                grads[own, pl.ds(number * own_cols, own_cols)], wbuf[number, rows, :], 1, 1
            )
            total = term if total is None else total + term
        return total

    input_copies = []
    for step in range(1, FSDP):
        peer = (fsdp + step) % FSDP
        gi_out[step - 1] = input_terms(peer).astype(BF16)
        input_copies.append(
            start(gi_out.at[step - 1], gi_in.at[step - 1], INPUT_SUMS + step - 1, at(d_fsdp=peer))
        )
    gi_own[...] = input_terms(fsdp)

    x2[own, :] = xs[own, :]
    pair_rows = pl.ds(pl.multiple_of((2 - core) * TOK, TOK), TOK)
    x2[pl.ds(TOK, TOK), :] = xs[pair_rows, :]
    core_grad.wait_recv()

    def weight_terms(owner):
        cols = pl.ds(pl.multiple_of(owner * TOK, TOK), TOK)
        return dot(x2[:, cols], grads[...], 0, 0)

    x_copies = []
    for step in range(1, XS):
        owner = ((x + step) % XS) * 2 + core
        gx_out[step - 1] = weight_terms(owner).astype(BF16)
        x_copies.append(
            start(gx_out.at[step - 1], gx_in.at[step - 1], SUM_X + step - 1, on_x(step))
        )
    total = weight_terms(lat)
    for copy in input_copies:
        copy.wait_recv()
    grad_input[...] = (
        gi_own[...] + gi_in[0].astype(F32) + gi_in[1].astype(F32) + gi_in[2].astype(F32)
    ).astype(BF16)
    for copy in x_copies:
        copy.wait_recv()
    r1[...] = total + (
        gx_in[0].astype(F32) + gx_in[1].astype(F32) + gx_in[2].astype(F32)
    )

    def both_halves(owner):
        low = r1[pl.ds(pl.multiple_of(owner * 8, 8), 8), :]
        high = r1[pl.ds(pl.multiple_of(YS * 8 + owner * 8, 8), 8), :]
        return jnp.concatenate([low, high], axis=0)

    y_copies = []
    for step in range(1, YS):
        gy_out[step - 1] = both_halves((y + step) % YS).astype(BF16)
        y_copies.append(
            start(gy_out.at[step - 1], gy_in.at[step - 1], SUM_Y + step - 1, on_y(step))
        )
    total = both_halves(y)
    for number, copy in enumerate(y_copies):
        copy.wait_recv()
        total = total + gy_in[number].astype(F32)
    r2[...] = total
    z_copy = start(
        r2.at[pl.ds(pl.multiple_of((1 - z_hi) * 8, 8), 8)], gz_in, SUM_Z, z_partner
    )
    z_copy.wait_recv()
    result = r2[pl.ds(pl.multiple_of(z_hi * 8, 8), 8), :] + gz_in[...]
    weight_scale = 1.0 / math.sqrt(TOK * LATS * LONS)
    for number in range(3):
        grad_weight[number] = result[:, number * own_cols : (number + 1) * own_cols] * weight_scale

    for copy in sent:
        copy.wait_send()


def shards(tokens, grad_out, weight):
    rows, cols, width = tokens.shape
    own_cols = grad_out.shape[2]
    three = weight.shape[0]
    anywhere = pl.BlockSpec(memory_space=pl.ANY)
    in_vmem = pl.BlockSpec(memory_space=pltpu.VMEM)
    total = three * own_cols
    grad_input, grad_weight = pl.pallas_call(
        kernel,
        out_shape=(
            jax.ShapeDtypeStruct((TOK, own_cols), BF16),
            jax.ShapeDtypeStruct((three, 8, own_cols), F32),
        ),
        in_specs=[anywhere] * 3,
        out_specs=(in_vmem, in_vmem),
        scratch_shapes=[
            pltpu.VMEM((EXT, width), BF16),
            pltpu.VMEM((EXT, own_cols), BF16),
            pltpu.VMEM((TOK, width + own_cols), BF16),
            pltpu.VMEM((three, width, own_cols), BF16),
            pltpu.VMEM((three, EXT, own_cols), BF16),
            pltpu.VMEM((EXT, TOK), F32),
            pltpu.VMEM((TOK, EXT), F32),
            pltpu.VMEM((32, TOK), F32),
            pltpu.VMEM((8, 16, TOK), F32),
            pltpu.VMEM((16, EXT), F32),
            pltpu.VMEM((2 * TOK, total), BF16),
            pltpu.VMEM((2 * TOK, width), BF16),
            pltpu.VMEM((three, TOK, own_cols), F32),
            pltpu.VMEM((TOK, own_cols), F32),
            pltpu.VMEM((FSDP - 1, TOK, own_cols), BF16),
            pltpu.VMEM((FSDP - 1, TOK, own_cols), BF16),
            pltpu.VMEM((XS - 1, TOK, total), BF16),
            pltpu.VMEM((XS - 1, TOK, total), BF16),
            pltpu.VMEM((TOK, total), F32),
            pltpu.VMEM((YS - 1, 16, total), BF16),
            pltpu.VMEM((YS - 1, 16, total), BF16),
            pltpu.VMEM((16, total), F32),
            pltpu.VMEM((8, total), F32),
            pltpu.SemaphoreType.DMA((COPIES,)),
            pltpu.SemaphoreType.DMA((COPIES,)),
            pltpu.SemaphoreType.DMA((3,)),
        ],
        compiler_params=pltpu.CompilerParams(
            collective_id=0, has_side_effects=True, vmem_limit_bytes=48 * 1024 * 1024
        ),
    )(tokens.reshape(TOK, width), grad_out.reshape(TOK, own_cols), weight)
    return grad_input.reshape(rows, cols, own_cols), grad_weight


def solution(mesh):
    placed = (P("lat", "lon", None), P("lat", "lon", "fsdp"), P(None, "fsdp", None))
    return jax.shard_map(
        shards,
        mesh=mesh,
        in_specs=placed,
        out_specs=(P("lat", "lon", "fsdp"), P(None, ("lat", "lon"), "fsdp")),
        check_vma=False,
    )
```

```python
import functools
import math

import jax
import jax.numpy as jnp
from jax import lax
from jax.experimental import pallas as pl
from jax.experimental.pallas import tpu as pltpu
from jax.sharding import PartitionSpec as P

HEADS = 16
RADIUS = 6
MESH = pl.DeviceIdType.MESH
BF16 = jnp.bfloat16
F32 = jnp.float32

ROWS, COLS = 8, 16
TOK = ROWS * COLS
BLOCKS = 6
EXT = BLOCKS * TOK
SLAB = RADIUS * ROWS
EAST, WEST = 0, 64
LATS, LONS, FSDP = 8, 16, 4
XS, YS, ZS = 4, 8, 8

NORTH_SOUTH, EAST_WEST, CORNERS = 0, 2, 4
GRADS = 8
WEIGHTS, CORE_WEIGHTS = 16, 19
STATS = 22
CORE_GRAD = 30
INPUT_SUMS = 32
SUM_X, SUM_Y, SUM_Z = 35, 41, 55
COPIES = 57


def dot(a, b, ca, cb, precision=None):
    return lax.dot_general(
        a, b, (((ca,), (cb,)), ((), ())), preferred_element_type=F32, precision=precision
    )


def place(block, spot):
    half = spot // 64
    inner = spot % 64
    side_col = inner // ROWS + jnp.where(half == 0, COLS, -RADIUS)
    is_tile = block < 3
    row = jnp.where(is_tile, spot // COLS, inner % ROWS)
    col = jnp.where(is_tile, spot % COLS, side_col)
    kind = block % 3
    shift = jnp.where(kind == 1, -ROWS, jnp.where(kind == 2, ROWS, 0))
    real = is_tile | (inner < SLAB)
    return row + shift, col, real


def bias_of(block, spot, own, lat):
    row, col, real = place(block, spot)
    own_row, own_col = own // COLS, own % COLS
    gap_r = row - own_row
    gap_c = col - own_col
    grid_row = lat * ROWS + row
    allowed = (
        real
        & (gap_r <= RADIUS)
        & (gap_r >= -RADIUS)
        & (gap_c <= RADIUS)
        & (gap_c >= -RADIUS)
        & (grid_row >= 0)
        & (grid_row < LATS * ROWS)
    )
    return jnp.where(allowed, 0.0, -jnp.inf).astype(F32)


def kernel(
    tokens,
    grad_out,
    weight,
    grad_input,
    grad_weight,
    xs,
    dos,
    packs,
    wbuf,
    qkv,
    bias_f,
    bias_b,
    stats,
    stats_in,
    stat_rows,
    grads,
    x2,
    acc,
    gi_own,
    gi_out,
    gi_in,
    gx_out,
    gx_in,
    r1,
    gy_out,
    gy_in,
    r2,
    gz_out,
    gz_in,
    send_sems,
    recv_sems,
    local_sems,
):
    lat = lax.axis_index("lat")
    lon = lax.axis_index("lon")
    fsdp = lax.axis_index("fsdp")
    x, core = lat // 2, lat % 2
    z_hi, y = lon // YS, lon % YS
    z = z_hi * FSDP + fsdp
    head_size = 64
    own_heads = HEADS // FSDP
    own_cols = own_heads * head_size
    width = FSDP * own_cols
    scale = 1.0 / math.sqrt(head_size)

    def at(*, d_lat=None, d_lon=None, d_fsdp=None):
        return (
            lat if d_lat is None else d_lat,
            lon if d_lon is None else d_lon,
            fsdp if d_fsdp is None else d_fsdp,
        )

    south_lat, north_lat = (lat + 1) % LATS, (lat + LATS - 1) % LATS
    east_lon, west_lon = (lon + 1) % LONS, (lon + LONS - 1) % LONS
    east_fsdp = jnp.where(y == YS - 1, FSDP - 1 - fsdp, fsdp)
    west_fsdp = jnp.where(y == 0, FSDP - 1 - fsdp, fsdp)
    south, north = at(d_lat=south_lat), at(d_lat=north_lat)
    east, west = at(d_lon=east_lon), at(d_lon=west_lon)
    east_copy = at(d_lon=east_lon, d_fsdp=east_fsdp)
    west_copy = at(d_lon=west_lon, d_fsdp=west_fsdp)
    other_core = at(d_lat=lat + 1 - 2 * core)

    def on_z(step):
        target = (z + step + ZS) % ZS
        return at(d_lon=(target // FSDP) * YS + y, d_fsdp=target % FSDP)

    def on_x(step):
        return at(d_lat=((x + step) % XS) * 2 + core)

    def on_y(step):
        return at(d_lon=z_hi * YS + (y + step) % YS)

    z_partner = at(d_lon=(1 - z_hi) * YS + y)
    corners = (
        at(d_lat=north_lat, d_lon=east_lon),
        at(d_lat=north_lat, d_lon=west_lon),
        at(d_lat=south_lat, d_lon=east_lon),
        at(d_lat=south_lat, d_lon=west_lon),
    )
    partners = [south, north, east, west, east_copy, west_copy, *corners]
    partners += [on_z(step) for step in (1, -1, 2, -2)]
    partners += [at(d_fsdp=(fsdp + step) % FSDP) for step in range(1, FSDP)]
    partners += [on_x(step) for step in range(1, XS)]
    partners += [on_y(step) for step in range(1, YS)]
    partners += [z_partner]

    barrier = pltpu.get_barrier_semaphore()
    for partner in partners:
        pl.semaphore_signal(barrier, inc=1, device_id=partner, device_id_type=MESH)

    own_tokens = pltpu.make_async_copy(tokens, xs.at[pl.ds(0, TOK)], local_sems.at[0])
    own_grads = pltpu.make_async_copy(grad_out, dos.at[pl.ds(0, TOK)], local_sems.at[1])
    own_start = pl.multiple_of(fsdp * own_cols, own_cols)
    own_weight = pltpu.make_async_copy(
        weight.at[:, :, pl.ds(own_start, own_cols)],
        wbuf.at[:, pl.ds(own_start, own_cols), :],
        local_sems.at[2],
    )
    own_tokens.start()
    own_grads.start()
    own_weight.start()

    def remote(src, dst, number, device):
        return pltpu.make_async_remote_copy(
            src_ref=src,
            dst_ref=dst,
            send_sem=send_sems.at[number],
            recv_sem=recv_sems.at[number],
            device_id=device,
            device_id_type=MESH,
        )

    own_tokens.wait()
    own_grads.wait()
    spot = lax.broadcasted_iota(jnp.int32, (TOK, TOK), 0)
    flat = lax.broadcasted_iota(jnp.int32, (TOK, TOK), 1)
    inner = spot % 64
    source = (inner % ROWS) * COLS + inner // ROWS + jnp.where(spot < 64, 0, COLS - RADIUS)
    picks = (inner < SLAB) & (flat == source)
    pick = jnp.where(picks, 1.0, 0.0).astype(F32)
    pick_16 = pick.astype(BF16)
    packs[:, pl.ds(0, width)] = dot(pick_16, xs[pl.ds(0, TOK), :], 1, 0).astype(BF16)
    packs[:, pl.ds(width, own_cols)] = dot(pick_16, dos[pl.ds(0, TOK), :], 1, 0).astype(BF16)
    pl.semaphore_wait(barrier, len(partners))

    sent = []

    def start(*args):
        copy = remote(*args)
        copy.start()
        sent.append(copy)
        return copy

    side_copies = []
    side = 3 * TOK
    for number, spot_at, token_device in ((0, EAST, west_copy), (1, WEST, east_copy)):
        side_copies.append(
            start(
                packs.at[pl.ds(spot_at, SLAB), pl.ds(0, width)],
                xs.at[pl.ds(side + spot_at, SLAB)],
                EAST_WEST + number,
                token_device,
            )
        )
    half_rows = own_cols // 2
    far = 2 - 4 * core
    weight_copies = []
    for number, step in enumerate((1, -1, far)):
        target = on_z(step)
        cols = pl.multiple_of(target[2] * own_cols, own_cols)
        rows = pl.multiple_of(fsdp * own_cols + core * half_rows, half_rows)
        weight_copies.append(
            start(
                weight.at[:, pl.ds(core * half_rows, half_rows), pl.ds(cols, own_cols)],
                wbuf.at[:, pl.ds(rows, half_rows), :],
                WEIGHTS + number,
                target,
            )
        )

    tile_copies = []
    for number, device, block in ((0, south, 1), (1, north, 2)):
        tile_copies.append(
            start(
                xs.at[pl.ds(0, TOK)], xs.at[pl.ds(block * TOK, TOK)], NORTH_SOUTH + number, device
            )
        )
    grad_tile_copies = []
    for number, device, block in ((0, south, 1), (1, north, 2)):
        grad_tile_copies.append(
            start(
                dos.at[pl.ds(0, TOK)],
                dos.at[pl.ds(block * TOK, TOK)],
                GRADS + NORTH_SOUTH + number,
                device,
            )
        )

    for block in range(3, BLOCKS):
        for spot_at in (EAST, WEST):
            unused = pl.ds(block * TOK + spot_at + SLAB, 64 - SLAB)
            xs[unused, :] = jnp.zeros((64 - SLAB, width), BF16)
            dos[unused, :] = jnp.zeros((64 - SLAB, own_cols), BF16)

    @pl.loop(0, BLOCKS)
    def _(block):
        first = pl.multiple_of(block * TOK, TOK)
        bias_f[pl.ds(first, TOK), :] = bias_of(block, spot, flat, lat)
        bias_b[:, pl.ds(first, TOK)] = bias_of(block, flat, spot, lat)

    corner_copies = []
    for number, spot_at in ((0, EAST), (1, WEST)):
        side_copies[number].wait_recv()
        for leg, (device, block) in enumerate(((south, 4), (north, 5))):
            corner_copies.append(
                start(
                    xs.at[pl.ds(side + spot_at, SLAB)],
                    xs.at[pl.ds(block * TOK + spot_at, SLAB)],
                    CORNERS + 2 * number + leg,
                    device,
                )
            )
    core_weight_copies = []
    for number, step in enumerate((-1, 1, -far)):
        weight_copies[number].wait_recv()
        origin = (fsdp + step + FSDP) % FSDP
        rows = pl.multiple_of(origin * own_cols + core * half_rows, half_rows)
        region = wbuf.at[:, pl.ds(rows, half_rows), :]
        core_weight_copies.append(start(region, region, CORE_WEIGHTS + number, other_core))
    grad_side_copies = []
    for number, spot_at, device in ((0, EAST, west), (1, WEST, east)):
        grad_side_copies.append(
            start(
                packs.at[pl.ds(spot_at, SLAB), pl.ds(width, own_cols)],
                dos.at[pl.ds(side + spot_at, SLAB)],
                GRADS + EAST_WEST + number,
                device,
            )
        )

    own_weight.wait()
    for copy in tile_copies + core_weight_copies + corner_copies:
        copy.wait_recv()

    @pl.loop(0, EXT // 256)
    def _(step):
        rows = pl.ds(pl.multiple_of(step * 256, 256), 256)
        block = xs[rows, :]
        for number in range(3):
            qkv[number, rows, :] = dot(block, wbuf[number], 1, 0).astype(BF16)

    lane = lax.broadcasted_iota(jnp.int32, (TOK, own_cols), 1) // head_size
    own = pl.ds(0, TOK)

    stats[pl.ds(3 * own_heads, own_heads), :] = jnp.zeros((own_heads, TOK), F32)

    @pl.loop(0, own_heads)
    def _(head):
        mine = lane == head
        query = jnp.where(mine, qkv[0, own, :], 0).astype(BF16)
        cotangent = jnp.where(mine, dos[own, :], 0).astype(BF16)
        scores = dot(qkv[1], query, 1, 1) * scale + bias_f[...]
        row_max = jnp.max(scores, axis=0, keepdims=True)
        prob = jnp.exp(scores - row_max)
        inv_sum = 1.0 / jnp.sum(prob, axis=0, keepdims=True)
        prob = prob * inv_sum
        grad_prob = dot(qkv[2], cotangent, 1, 1)
        delta = jnp.sum(prob * grad_prob, axis=0, keepdims=True)
        grad_score = (scale * (prob * (grad_prob - delta))).astype(BF16)
        part = dot(grad_score, qkv[1], 0, 0)
        acc[0] = jnp.where(mine, part, acc[0])
        stats[pl.ds(head, 1), :] = row_max
        stats[pl.ds(own_heads + head, 1), :] = inv_sum
        stats[pl.ds(2 * own_heads + head, 1), :] = delta

    stats[pl.ds(16, 16), :] = dot(
        stats[pl.ds(0, 16), :], pick, 1, 1, precision=lax.Precision.HIGHEST
    )
    tile_stats = stats.at[pl.ds(0, 16)]
    side_stats = stats.at[pl.ds(16, 16)]
    stat_copies = []
    for number, (src, device) in enumerate(
        (
            (tile_stats, south),
            (tile_stats, north),
            (side_stats, west),
            (side_stats, east),
            (side_stats, corners[3]),
            (side_stats, corners[2]),
            (side_stats, corners[1]),
            (side_stats, corners[0]),
        )
    ):
        stat_copies.append(start(src, stats_in.at[number], STATS + number, device))

    parts = ((0, own_cols), (own_cols, 2 * own_cols))
    core_copies = []
    x_copies = [[], []]
    y_copies = [[], []]
    z_copies = []

    def share_with_core(part):
        cols = pl.ds(*parts[part])
        return start(
            grads.at[own, cols],
            grads.at[pl.ds(TOK, TOK), cols],
            CORE_GRAD + part,
            other_core,
        )

    def input_terms(owner, numbers):
        rows = pl.ds(pl.multiple_of(owner * own_cols, own_cols), own_cols)
        total = None
        for number in numbers:
            term = dot(
                grads[own, pl.ds(number * own_cols, own_cols)], wbuf[number, rows, :], 1, 1
            )
            total = term if total is None else total + term
        return total

    def send_x(part):
        core_copies[part].wait_recv()
        cols = pl.ds(*parts[part])

        def terms(owner):
            rows = pl.ds(pl.multiple_of(owner * TOK, TOK), TOK)
            return dot(x2[:, rows], grads[:, cols], 0, 0)

        for step in range(1, XS):
            gx_out[step - 1, :, cols] = terms(((x + step) % XS) * 2 + core).astype(BF16)
            x_copies[part].append(
                start(
                    gx_out.at[step - 1, :, cols],
                    gx_in.at[step - 1, :, cols],
                    SUM_X + (XS - 1) * part + step - 1,
                    on_x(step),
                )
            )
        r1[:, cols] = terms(lat)

    def send_y(part):
        cols = pl.ds(*parts[part])
        for copy in x_copies[part]:
            copy.wait_recv()
        total = r1[:, cols]
        for number in range(XS - 1):
            total = total + gx_in[number, :, cols].astype(F32)
        r1[:, cols] = total
        for step in range(1, YS):
            gy_out[step - 1, :, cols] = both_halves((y + step) % YS, cols).astype(BF16)
            y_copies[part].append(
                start(
                    gy_out.at[step - 1, :, cols],
                    gy_in.at[step - 1, :, cols],
                    SUM_Y + (YS - 1) * part + step - 1,
                    on_y(step),
                )
            )

    def both_halves(owner, cols):
        low = r1[pl.ds(pl.multiple_of(owner * 8, 8), 8), cols]
        high = r1[pl.ds(pl.multiple_of(YS * 8 + owner * 8, 8), 8), cols]
        return jnp.concatenate([low, high], axis=0)

    def send_z(part):
        first, count = parts[part]
        cols = pl.ds(first, count)
        half = count // 2
        total = both_halves(y, cols)
        for number, copy in enumerate(y_copies[part]):
            copy.wait_recv()
            total = total + gy_in[number, :, cols].astype(F32)
        r2[:, cols] = total
        rows = pl.ds(pl.multiple_of((1 - z_hi) * 8, 8), 8)
        folded = pl.ds(first // 2, half)
        gz_out[:, folded] = jnp.concatenate(
            [r2[rows, pl.ds(first, half)], r2[rows, pl.ds(first + half, half)]], axis=0
        ).astype(BF16)
        z_copies.append(
            start(gz_out.at[:, folded], gz_in.at[:, folded], SUM_Z + part, z_partner)
        )

    def finish(part):
        first, count = parts[part]
        half = count // 2
        z_copies[part].wait_recv()
        other = gz_in[:, pl.ds(first // 2, half)].astype(F32)
        own_rows = pl.ds(pl.multiple_of(z_hi * 8, 8), 8)
        total = r2[own_rows, pl.ds(first, count)]
        total = (total + jnp.concatenate([other[:8], other[8:]], axis=1)) * weight_scale
        for number in range(count // own_cols):
            grad_weight[first // own_cols + number] = total[
                :, number * own_cols : (number + 1) * own_cols
            ]

    weight_scale = 1.0 / math.sqrt(TOK * LATS * LONS)
    grads[own, pl.ds(0, own_cols)] = acc[0].astype(BF16)
    core_copies.append(share_with_core(0))
    x2[own, :] = xs[own, :]
    pair_rows = pl.ds(pl.multiple_of((2 - core) * TOK, TOK), TOK)
    x2[pl.ds(TOK, TOK), :] = xs[pair_rows, :]
    for step in range(FSDP):
        gi_own[step] = input_terms((fsdp + step) % FSDP, (0,))
    send_x(0)
    grad_corner_copies = []
    for number, spot_at in ((0, EAST), (1, WEST)):
        grad_side_copies[number].wait_recv()
        for leg, (device, block) in enumerate(((south, 4), (north, 5))):
            grad_corner_copies.append(
                start(
                    dos.at[pl.ds(side + spot_at, SLAB)],
                    dos.at[pl.ds(block * TOK + spot_at, SLAB)],
                    GRADS + CORNERS + 2 * number + leg,
                    device,
                )
            )
    for copy in grad_tile_copies + grad_corner_copies + stat_copies:
        copy.wait_recv()
    half_lane = lax.broadcasted_iota(jnp.int32, (16, TOK), 1) < 64
    stat_rows[:, pl.ds(0, TOK)] = stats[pl.ds(0, 16), :]
    stat_rows[:, pl.ds(TOK, TOK)] = stats_in[0]
    stat_rows[:, pl.ds(2 * TOK, TOK)] = stats_in[1]
    for block in range(3):
        first = 2 + 2 * block
        stat_rows[:, pl.ds((3 + block) * TOK, TOK)] = jnp.where(
            half_lane, stats_in[first], stats_in[first + 1]
        )

    @pl.loop(0, own_heads)
    def _(head):
        mine = lane == head
        key = jnp.where(mine, qkv[1, own, :], 0).astype(BF16)
        value = jnp.where(mine, qkv[2, own, :], 0).astype(BF16)
        row_max = stat_rows[pl.ds(head, 1), :]
        inv_sum = stat_rows[pl.ds(own_heads + head, 1), :]
        delta = stat_rows[pl.ds(2 * own_heads + head, 1), :]
        scores = dot(key, qkv[0], 1, 1) * scale + bias_b[...]
        prob = jnp.exp(jnp.minimum(scores - row_max, 0.0)) * inv_sum
        grad_prob = dot(value, dos[...], 1, 1)
        grad_score = (scale * (prob * (grad_prob - delta))).astype(BF16)
        acc[1] = jnp.where(mine, dot(grad_score, qkv[0], 1, 0), acc[1])
        acc[2] = jnp.where(mine, dot(prob.astype(BF16), dos[...], 1, 0), acc[2])

    for number in (1, 2):
        grads[own, pl.ds(number * own_cols, own_cols)] = acc[number].astype(BF16)
    core_copies.append(share_with_core(1))

    input_copies = []
    for step in range(1, FSDP):
        peer = (fsdp + step) % FSDP
        gi_out[step - 1] = (gi_own[step] + input_terms(peer, (1, 2))).astype(BF16)
        input_copies.append(
            start(gi_out.at[step - 1], gi_in.at[step - 1], INPUT_SUMS + step - 1, at(d_fsdp=peer))
        )
    gi_own[0] = gi_own[0] + input_terms(fsdp, (1, 2))
    send_x(1)
    send_y(0)
    for copy in input_copies:
        copy.wait_recv()
    grad_input[...] = (
        gi_own[0] + gi_in[0].astype(F32) + gi_in[1].astype(F32) + gi_in[2].astype(F32)
    ).astype(BF16)
    send_z(0)
    send_y(1)
    send_z(1)
    finish(0)
    finish(1)

    for copy in sent:
        copy.wait_send()


def shards(tokens, grad_out, weight):
    rows, cols, width = tokens.shape
    own_cols = grad_out.shape[2]
    three = weight.shape[0]
    anywhere = pl.BlockSpec(memory_space=pl.ANY)
    in_vmem = pl.BlockSpec(memory_space=pltpu.VMEM)
    total = three * own_cols
    grad_input, grad_weight = pl.pallas_call(
        kernel,
        out_shape=(
            jax.ShapeDtypeStruct((TOK, own_cols), BF16),
            jax.ShapeDtypeStruct((three, 8, own_cols), F32),
        ),
        in_specs=[anywhere] * 3,
        out_specs=(in_vmem, in_vmem),
        scratch_shapes=[
            pltpu.VMEM((EXT, width), BF16),
            pltpu.VMEM((EXT, own_cols), BF16),
            pltpu.VMEM((TOK, width + own_cols), BF16),
            pltpu.VMEM((three, width, own_cols), BF16),
            pltpu.VMEM((three, EXT, own_cols), BF16),
            pltpu.VMEM((EXT, TOK), F32),
            pltpu.VMEM((TOK, EXT), F32),
            pltpu.VMEM((32, TOK), F32),
            pltpu.VMEM((8, 16, TOK), F32),
            pltpu.VMEM((16, EXT), F32),
            pltpu.VMEM((2 * TOK, total), BF16),
            pltpu.VMEM((2 * TOK, width), BF16),
            pltpu.VMEM((three, TOK, own_cols), F32),
            pltpu.VMEM((FSDP, TOK, own_cols), F32),
            pltpu.VMEM((FSDP - 1, TOK, own_cols), BF16),
            pltpu.VMEM((FSDP - 1, TOK, own_cols), BF16),
            pltpu.VMEM((XS - 1, TOK, total), BF16),
            pltpu.VMEM((XS - 1, TOK, total), BF16),
            pltpu.VMEM((TOK, total), F32),
            pltpu.VMEM((YS - 1, 16, total), BF16),
            pltpu.VMEM((YS - 1, 16, total), BF16),
            pltpu.VMEM((16, total), F32),
            pltpu.VMEM((16, total // 2), BF16),
            pltpu.VMEM((16, total // 2), BF16),
            pltpu.SemaphoreType.DMA((COPIES,)),
            pltpu.SemaphoreType.DMA((COPIES,)),
            pltpu.SemaphoreType.DMA((3,)),
        ],
        compiler_params=pltpu.CompilerParams(
            collective_id=0, has_side_effects=True, vmem_limit_bytes=63 * 1024 * 1024
        ),
    )(tokens.reshape(TOK, width), grad_out.reshape(TOK, own_cols), weight)
    return grad_input.reshape(rows, cols, own_cols), grad_weight


def solution(mesh):
    placed = (P("lat", "lon", None), P("lat", "lon", "fsdp"), P(None, "fsdp", None))
    return jax.shard_map(
        shards,
        mesh=mesh,
        in_specs=placed,
        out_specs=(P("lat", "lon", "fsdp"), P(None, ("lat", "lon"), "fsdp")),
        check_vma=False,
    )
```

```python
import functools
import math

import jax
import jax.numpy as jnp
from jax import lax
from jax.experimental import pallas as pl
from jax.experimental.pallas import tpu as pltpu
from jax.sharding import PartitionSpec as P

HEADS = 16
RADIUS = 6
MESH = pl.DeviceIdType.MESH
BF16 = jnp.bfloat16
F32 = jnp.float32

ROWS, COLS = 8, 16
TOK = ROWS * COLS
BLOCKS = 6
EXT = BLOCKS * TOK
SLAB = RADIUS * ROWS
EAST, WEST = 0, 64
LATS, LONS, FSDP = 8, 16, 4
XS, YS, ZS = 4, 8, 8

NORTH_SOUTH, EAST_WEST, CORNERS = 0, 2, 4
GRADS = 8
WEIGHTS, SIDE_WEIGHTS, CORE_WEIGHTS = 16, 19, 25
STATS = 31
CORE_GRAD = 39
INPUT_SUMS = 42
SUM_X, SUM_Y, SUM_Z = 45, 54, 75
COPIES = 78


def dot(a, b, ca, cb, precision=None):
    return lax.dot_general(
        a, b, (((ca,), (cb,)), ((), ())), preferred_element_type=F32, precision=precision
    )


def place(block, spot):
    half = spot // 64
    inner = spot % 64
    side_col = inner // ROWS + jnp.where(half == 0, COLS, -RADIUS)
    is_tile = block < 3
    row = jnp.where(is_tile, spot // COLS, inner % ROWS)
    col = jnp.where(is_tile, spot % COLS, side_col)
    kind = block % 3
    shift = jnp.where(kind == 1, -ROWS, jnp.where(kind == 2, ROWS, 0))
    real = is_tile | (inner < SLAB)
    return row + shift, col, real


def bias_of(block, spot, own, lat):
    row, col, real = place(block, spot)
    own_row, own_col = own // COLS, own % COLS
    gap_r = row - own_row
    gap_c = col - own_col
    grid_row = lat * ROWS + row
    allowed = (
        real
        & (gap_r <= RADIUS)
        & (gap_r >= -RADIUS)
        & (gap_c <= RADIUS)
        & (gap_c >= -RADIUS)
        & (grid_row >= 0)
        & (grid_row < LATS * ROWS)
    )
    return jnp.where(allowed, 0.0, -jnp.inf).astype(F32)


def kernel(
    tokens,
    grad_out,
    weight,
    grad_input,
    grad_weight,
    xs,
    dos,
    packs,
    wbuf,
    qkv,
    bias_f,
    bias_b,
    stats,
    stats_in,
    stat_rows,
    grads,
    xt,
    probs,
    acc,
    gi_own,
    gi_out,
    gi_in,
    gx_out,
    gx_in,
    r1,
    gy_out,
    gy_in,
    r2,
    gz_out,
    gz_in,
    send_sems,
    recv_sems,
    local_sems,
):
    lat = lax.axis_index("lat")
    lon = lax.axis_index("lon")
    fsdp = lax.axis_index("fsdp")
    x, core = lat // 2, lat % 2
    z_hi, y = lon // YS, lon % YS
    z = z_hi * FSDP + fsdp
    head_size = 64
    own_heads = HEADS // FSDP
    own_cols = own_heads * head_size
    width = FSDP * own_cols
    scale = 1.0 / math.sqrt(head_size)

    def at(*, d_lat=None, d_lon=None, d_fsdp=None):
        return (
            lat if d_lat is None else d_lat,
            lon if d_lon is None else d_lon,
            fsdp if d_fsdp is None else d_fsdp,
        )

    south_lat, north_lat = (lat + 1) % LATS, (lat + LATS - 1) % LATS
    east_lon, west_lon = (lon + 1) % LONS, (lon + LONS - 1) % LONS
    east_fsdp = jnp.where(y == YS - 1, FSDP - 1 - fsdp, fsdp)
    west_fsdp = jnp.where(y == 0, FSDP - 1 - fsdp, fsdp)
    south, north = at(d_lat=south_lat), at(d_lat=north_lat)
    east, west = at(d_lon=east_lon), at(d_lon=west_lon)
    east_copy = at(d_lon=east_lon, d_fsdp=east_fsdp)
    west_copy = at(d_lon=west_lon, d_fsdp=west_fsdp)
    other_core = at(d_lat=lat + 1 - 2 * core)

    def on_z(step):
        target = (z + step + ZS) % ZS
        return at(d_lon=(target // FSDP) * YS + y, d_fsdp=target % FSDP)

    def on_x(step):
        return at(d_lat=((x + step) % XS) * 2 + core)

    def on_y(step):
        return at(d_lon=z_hi * YS + (y + step) % YS)

    z_partner = at(d_lon=(1 - z_hi) * YS + y)
    corners = (
        at(d_lat=north_lat, d_lon=east_lon),
        at(d_lat=north_lat, d_lon=west_lon),
        at(d_lat=south_lat, d_lon=east_lon),
        at(d_lat=south_lat, d_lon=west_lon),
    )
    partners = [south, north, east, west, east_copy, west_copy, *corners]
    partners += [on_z(step) for step in (1, -1, 2, -2)]
    partners += [at(d_fsdp=(fsdp + step) % FSDP) for step in range(1, FSDP)]
    partners += [on_x(step) for step in range(1, XS)]
    partners += [on_y(step) for step in range(1, YS)]
    partners += [z_partner]

    barrier = pltpu.get_barrier_semaphore()
    for partner in partners:
        pl.semaphore_signal(barrier, inc=1, device_id=partner, device_id_type=MESH)

    own_tokens = pltpu.make_async_copy(tokens, xs.at[pl.ds(0, TOK)], local_sems.at[0])
    own_grads = pltpu.make_async_copy(grad_out, dos.at[pl.ds(0, TOK)], local_sems.at[1])
    own_start = pl.multiple_of(fsdp * own_cols, own_cols)
    own_weight = pltpu.make_async_copy(
        weight.at[:, :, pl.ds(own_start, own_cols)],
        wbuf.at[:, pl.ds(own_start, own_cols), :],
        local_sems.at[2],
    )
    own_tokens.start()
    own_grads.start()
    own_weight.start()

    def remote(src, dst, number, device):
        return pltpu.make_async_remote_copy(
            src_ref=src,
            dst_ref=dst,
            send_sem=send_sems.at[number],
            recv_sem=recv_sems.at[number],
            device_id=device,
            device_id_type=MESH,
        )

    pl.semaphore_wait(barrier, len(partners))

    sent = []

    def start(*args):
        copy = remote(*args)
        copy.start()
        sent.append(copy)
        return copy

    half_rows = own_cols // 2
    quarter = half_rows // 2
    eighth = quarter // 2
    parity = y % 2
    far = 2 - 4 * core
    mine_at = core * half_rows + parity * quarter
    other_at = core * half_rows + (1 - parity) * quarter

    def weight_rows(origin, offset, count):
        first = pl.multiple_of(origin * own_cols + offset, eighth)
        return wbuf.at[:, pl.ds(first, count), :]

    weight_copies = []
    for number, step in enumerate((1, -1, far)):
        target = on_z(step)
        cols = pl.multiple_of(target[2] * own_cols, own_cols)
        weight_copies.append(
            start(
                weight.at[
                    :, pl.ds(pl.multiple_of(mine_at, quarter), quarter), pl.ds(cols, own_cols)
                ],
                weight_rows(fsdp, mine_at, quarter),
                WEIGHTS + number,
                target,
            )
        )

    tile_copies = []
    for number, device, block in ((0, south, 1), (1, north, 2)):
        tile_copies.append(
            start(
                tokens, xs.at[pl.ds(block * TOK, TOK)], NORTH_SOUTH + number, device
            )
        )
    grad_tile_copies = []
    for number, device, block in ((0, south, 1), (1, north, 2)):
        grad_tile_copies.append(
            start(
                grad_out,
                dos.at[pl.ds(block * TOK, TOK)],
                GRADS + NORTH_SOUTH + number,
                device,
            )
        )

    own_tokens.wait()
    own_grads.wait()
    spot = lax.broadcasted_iota(jnp.int32, (TOK, TOK), 0)
    flat = lax.broadcasted_iota(jnp.int32, (TOK, TOK), 1)
    inner = spot % 64
    source = (inner % ROWS) * COLS + inner // ROWS + jnp.where(spot < 64, 0, COLS - RADIUS)
    picks = (inner < SLAB) & (flat == source)
    pick = jnp.where(picks, 1.0, 0.0).astype(F32)
    pick_16 = pick.astype(BF16)
    packs[:, pl.ds(0, width)] = dot(pick_16, xs[pl.ds(0, TOK), :], 1, 0).astype(BF16)
    packs[:, pl.ds(width, own_cols)] = dot(pick_16, dos[pl.ds(0, TOK), :], 1, 0).astype(BF16)
    side_copies = []
    side = 3 * TOK
    for number, spot_at, token_device in ((0, EAST, west_copy), (1, WEST, east_copy)):
        side_copies.append(
            start(
                packs.at[pl.ds(spot_at, SLAB), pl.ds(0, width)],
                xs.at[pl.ds(side + spot_at, SLAB)],
                EAST_WEST + number,
                token_device,
            )
        )
    xt[:, pl.ds(0, TOK)] = xs[pl.ds(0, TOK), :].T

    for block in range(3, BLOCKS):
        for spot_at in (EAST, WEST):
            unused = pl.ds(block * TOK + spot_at + SLAB, 64 - SLAB)
            xs[unused, :] = jnp.zeros((64 - SLAB, width), BF16)
            dos[unused, :] = jnp.zeros((64 - SLAB, own_cols), BF16)

    @pl.loop(0, BLOCKS)
    def _(block):
        first = pl.multiple_of(block * TOK, TOK)
        bias_f[pl.ds(first, TOK), :] = bias_of(block, spot, flat, lat)
        bias_b[:, pl.ds(first, TOK)] = bias_of(block, flat, spot, lat)

    side_weight_copies = []
    core_weight_copies = []
    origins = [(fsdp + step + FSDP) % FSDP for step in (-1, 1, -far)]
    for number, origin in enumerate(origins):
        weight_copies[number].wait_recv()
        for leg, step in enumerate((1, -1)):
            region = weight_rows(origin, mine_at + leg * eighth, eighth)
            side_weight_copies.append(
                start(region, region, SIDE_WEIGHTS + 2 * number + leg, on_y(step))
            )
        region = weight_rows(origin, mine_at, quarter)
        core_weight_copies.append(start(region, region, CORE_WEIGHTS + 2 * number, other_core))
    corner_copies = []
    for number, spot_at in ((0, EAST), (1, WEST)):
        side_copies[number].wait_recv()
        for leg, (device, block) in enumerate(((south, 4), (north, 5))):
            corner_copies.append(
                start(
                    xs.at[pl.ds(side + spot_at, SLAB)],
                    xs.at[pl.ds(block * TOK + spot_at, SLAB)],
                    CORNERS + 2 * number + leg,
                    device,
                )
            )
    grad_side_copies = []
    for number, spot_at, device in ((0, EAST, west), (1, WEST, east)):
        grad_side_copies.append(
            start(
                packs.at[pl.ds(spot_at, SLAB), pl.ds(width, own_cols)],
                dos.at[pl.ds(side + spot_at, SLAB)],
                GRADS + EAST_WEST + number,
                device,
            )
        )

    for copy in tile_copies:
        copy.wait_recv()
    pair_rows = pl.ds(pl.multiple_of((2 - core) * TOK, TOK), TOK)
    xt[:, pl.ds(TOK, TOK)] = xs[pair_rows, :].T
    for number, origin in enumerate(origins):
        for leg in range(2):
            side_weight_copies[2 * number + leg].wait_recv()
        region = weight_rows(origin, other_at, quarter)
        core_weight_copies.append(start(region, region, CORE_WEIGHTS + 2 * number + 1, other_core))
    own_weight.wait()
    for copy in core_weight_copies + corner_copies:
        copy.wait_recv()

    @pl.loop(0, EXT // 256)
    def _(step):
        rows = pl.ds(pl.multiple_of(step * 256, 256), 256)
        block = xs[rows, :]
        for number in range(3):
            qkv[number, rows, :] = dot(block, wbuf[number], 1, 0).astype(BF16)

    lane = lax.broadcasted_iota(jnp.int32, (TOK, own_cols), 1) // head_size
    own = pl.ds(0, TOK)

    stats[pl.ds(3 * own_heads, own_heads), :] = jnp.zeros((own_heads, TOK), F32)

    @pl.loop(0, own_heads)
    def _(head):
        mine = lane == head
        query = jnp.where(mine, qkv[0, own, :], 0).astype(BF16)
        cotangent = jnp.where(mine, dos[own, :], 0).astype(BF16)
        scores = dot(qkv[1], query, 1, 1) * scale + bias_f[...]
        row_max = jnp.max(scores, axis=0, keepdims=True)
        prob = jnp.exp(scores - row_max)
        inv_sum = 1.0 / jnp.sum(prob, axis=0, keepdims=True)
        prob = prob * inv_sum
        grad_prob = dot(qkv[2], cotangent, 1, 1)
        delta = jnp.sum(prob * grad_prob, axis=0, keepdims=True)
        grad_score = (scale * (prob * (grad_prob - delta))).astype(BF16)
        part = dot(grad_score, qkv[1], 0, 0)
        acc[0] = jnp.where(mine, part, acc[0])
        stats[pl.ds(head, 1), :] = row_max
        stats[pl.ds(own_heads + head, 1), :] = inv_sum
        stats[pl.ds(2 * own_heads + head, 1), :] = delta

    stats[pl.ds(16, 16), :] = dot(
        stats[pl.ds(0, 16), :], pick, 1, 1, precision=lax.Precision.HIGHEST
    )
    tile_stats = stats.at[pl.ds(0, 16)]
    side_stats = stats.at[pl.ds(16, 16)]
    stat_copies = []
    for number, (src, device) in enumerate(
        (
            (tile_stats, south),
            (tile_stats, north),
            (side_stats, west),
            (side_stats, east),
            (side_stats, corners[3]),
            (side_stats, corners[2]),
            (side_stats, corners[1]),
            (side_stats, corners[0]),
        )
    ):
        stat_copies.append(start(src, stats_in.at[number], STATS + number, device))

    parts = tuple((number * own_cols, own_cols) for number in (0, 2, 1))
    core_copies = []
    x_copies = [[], [], []]
    y_copies = [[], [], []]
    z_copies = []

    def share_with_core(part):
        cols = pl.ds(*parts[part])
        return start(
            grads.at[own, cols],
            grads.at[pl.ds(TOK, TOK), cols],
            CORE_GRAD + part,
            other_core,
        )

    def input_terms(owner, numbers):
        rows = pl.ds(pl.multiple_of(owner * own_cols, own_cols), own_cols)
        total = None
        for number in numbers:
            term = dot(
                grads[own, pl.ds(number * own_cols, own_cols)], wbuf[number, rows, :], 1, 1
            )
            total = term if total is None else total + term
        return total

    def send_x(part):
        core_copies[part].wait_recv()
        cols = pl.ds(*parts[part])

        def terms(owner):
            rows = pl.ds(pl.multiple_of(owner * TOK, TOK), TOK)
            return dot(xt[rows, :], grads[:, cols], 1, 0)

        for step in range(1, XS):
            gx_out[step - 1, :, cols] = terms(((x + step) % XS) * 2 + core).astype(BF16)
            x_copies[part].append(
                start(
                    gx_out.at[step - 1, :, cols],
                    gx_in.at[step - 1, :, cols],
                    SUM_X + (XS - 1) * part + step - 1,
                    on_x(step),
                )
            )
        r1[:, cols] = terms(lat)

    def send_y(part):
        cols = pl.ds(*parts[part])
        for copy in x_copies[part]:
            copy.wait_recv()
        total = r1[:, cols]
        for number in range(XS - 1):
            total = total + gx_in[number, :, cols].astype(F32)
        r1[:, cols] = total
        for step in range(1, YS):
            gy_out[step - 1, :, cols] = both_halves((y + step) % YS, cols).astype(BF16)
            y_copies[part].append(
                start(
                    gy_out.at[step - 1, :, cols],
                    gy_in.at[step - 1, :, cols],
                    SUM_Y + (YS - 1) * part + step - 1,
                    on_y(step),
                )
            )

    def both_halves(owner, cols):
        low = r1[pl.ds(pl.multiple_of(owner * 8, 8), 8), cols]
        high = r1[pl.ds(pl.multiple_of(YS * 8 + owner * 8, 8), 8), cols]
        return jnp.concatenate([low, high], axis=0)

    def send_z(part):
        first, count = parts[part]
        cols = pl.ds(first, count)
        half = count // 2
        total = both_halves(y, cols)
        for number, copy in enumerate(y_copies[part]):
            copy.wait_recv()
            total = total + gy_in[number, :, cols].astype(F32)
        r2[:, cols] = total
        rows = pl.ds(pl.multiple_of((1 - z_hi) * 8, 8), 8)
        folded = pl.ds(first // 2, half)
        gz_out[:, folded] = jnp.concatenate(
            [r2[rows, pl.ds(first, half)], r2[rows, pl.ds(first + half, half)]], axis=0
        ).astype(BF16)
        z_copies.append(
            start(gz_out.at[:, folded], gz_in.at[:, folded], SUM_Z + part, z_partner)
        )

    def finish(part):
        first, count = parts[part]
        half = count // 2
        z_copies[part].wait_recv()
        other = gz_in[:, pl.ds(first // 2, half)].astype(F32)
        own_rows = pl.ds(pl.multiple_of(z_hi * 8, 8), 8)
        total = r2[own_rows, pl.ds(first, count)]
        total = (total + jnp.concatenate([other[:8], other[8:]], axis=1)) * weight_scale
        for number in range(count // own_cols):
            grad_weight[first // own_cols + number] = total[
                :, number * own_cols : (number + 1) * own_cols
            ]

    weight_scale = 1.0 / math.sqrt(TOK * LATS * LONS)
    grads[own, pl.ds(0, own_cols)] = acc[0].astype(BF16)
    core_copies.append(share_with_core(0))
    for step in range(FSDP):
        gi_own[step] = input_terms((fsdp + step) % FSDP, (0,))
    send_x(0)
    grad_corner_copies = []
    for number, spot_at in ((0, EAST), (1, WEST)):
        grad_side_copies[number].wait_recv()
        for leg, (device, block) in enumerate(((south, 4), (north, 5))):
            grad_corner_copies.append(
                start(
                    dos.at[pl.ds(side + spot_at, SLAB)],
                    dos.at[pl.ds(block * TOK + spot_at, SLAB)],
                    GRADS + CORNERS + 2 * number + leg,
                    device,
                )
            )
    for copy in grad_tile_copies + grad_corner_copies + stat_copies:
        copy.wait_recv()
    half_lane = lax.broadcasted_iota(jnp.int32, (16, TOK), 1) < 64
    stat_rows[:, pl.ds(0, TOK)] = stats[pl.ds(0, 16), :]
    stat_rows[:, pl.ds(TOK, TOK)] = stats_in[0]
    stat_rows[:, pl.ds(2 * TOK, TOK)] = stats_in[1]
    for block in range(3):
        first = 2 + 2 * block
        stat_rows[:, pl.ds((3 + block) * TOK, TOK)] = jnp.where(
            half_lane, stats_in[first], stats_in[first + 1]
        )

    @pl.loop(0, own_heads)
    def _(head):
        mine = lane == head
        key = jnp.where(mine, qkv[1, own, :], 0).astype(BF16)
        row_max = stat_rows[pl.ds(head, 1), :]
        inv_sum = stat_rows[pl.ds(own_heads + head, 1), :]
        scores = dot(key, qkv[0], 1, 1) * scale + bias_b[...]
        prob = jnp.exp(jnp.minimum(scores - row_max, 0.0)) * inv_sum
        probs[head] = prob
        acc[2] = jnp.where(mine, dot(prob.astype(BF16), dos[...], 1, 0), acc[2])

    grads[own, pl.ds(2 * own_cols, own_cols)] = acc[2].astype(BF16)
    core_copies.append(share_with_core(1))

    @pl.loop(0, own_heads)
    def _(head):
        mine = lane == head
        value = jnp.where(mine, qkv[2, own, :], 0).astype(BF16)
        delta = stat_rows[pl.ds(2 * own_heads + head, 1), :]
        grad_prob = dot(value, dos[...], 1, 1)
        grad_score = (scale * (probs[head] * (grad_prob - delta))).astype(BF16)
        acc[1] = jnp.where(mine, dot(grad_score, qkv[0], 1, 0), acc[1])

    grads[own, pl.ds(own_cols, own_cols)] = acc[1].astype(BF16)
    core_copies.append(share_with_core(2))
    send_x(1)

    input_copies = []
    for step in range(1, FSDP):
        peer = (fsdp + step) % FSDP
        gi_out[step - 1] = (gi_own[step] + input_terms(peer, (1, 2))).astype(BF16)
        input_copies.append(
            start(gi_out.at[step - 1], gi_in.at[step - 1], INPUT_SUMS + step - 1, at(d_fsdp=peer))
        )
    send_x(2)
    send_y(0)
    gi_own[0] = gi_own[0] + input_terms(fsdp, (1, 2))
    send_y(1)
    send_z(0)
    for copy in input_copies:
        copy.wait_recv()
    grad_input[...] = (
        gi_own[0] + gi_in[0].astype(F32) + gi_in[1].astype(F32) + gi_in[2].astype(F32)
    ).astype(BF16)
    send_y(2)
    send_z(1)
    finish(0)
    send_z(2)
    finish(1)
    finish(2)

    for copy in sent:
        copy.wait_send()


def shards(tokens, grad_out, weight):
    rows, cols, width = tokens.shape
    own_cols = grad_out.shape[2]
    three = weight.shape[0]
    anywhere = pl.BlockSpec(memory_space=pl.ANY)
    in_vmem = pl.BlockSpec(memory_space=pltpu.VMEM)
    total = three * own_cols
    grad_input, grad_weight = pl.pallas_call(
        kernel,
        out_shape=(
            jax.ShapeDtypeStruct((TOK, own_cols), BF16),
            jax.ShapeDtypeStruct((three, 8, own_cols), F32),
        ),
        in_specs=[anywhere] * 3,
        out_specs=(in_vmem, in_vmem),
        scratch_shapes=[
            pltpu.VMEM((EXT, width), BF16),
            pltpu.VMEM((EXT, own_cols), BF16),
            pltpu.VMEM((TOK, width + own_cols), BF16),
            pltpu.VMEM((three, width, own_cols), BF16),
            pltpu.VMEM((three, EXT, own_cols), BF16),
            pltpu.VMEM((EXT, TOK), F32),
            pltpu.VMEM((TOK, EXT), F32),
            pltpu.VMEM((32, TOK), F32),
            pltpu.VMEM((8, 16, TOK), F32),
            pltpu.VMEM((16, EXT), F32),
            pltpu.VMEM((2 * TOK, total), BF16),
            pltpu.VMEM((width, 2 * TOK), BF16),
            pltpu.VMEM((own_cols // 64, TOK, EXT), F32),
            pltpu.VMEM((three, TOK, own_cols), F32),
            pltpu.VMEM((FSDP, TOK, own_cols), F32),
            pltpu.VMEM((FSDP - 1, TOK, own_cols), BF16),
            pltpu.VMEM((FSDP - 1, TOK, own_cols), BF16),
            pltpu.VMEM((XS - 1, TOK, total), BF16),
            pltpu.VMEM((XS - 1, TOK, total), BF16),
            pltpu.VMEM((TOK, total), F32),
            pltpu.VMEM((YS - 1, 16, total), BF16),
            pltpu.VMEM((YS - 1, 16, total), BF16),
            pltpu.VMEM((16, total), F32),
            pltpu.VMEM((16, total // 2), BF16),
            pltpu.VMEM((16, total // 2), BF16),
            pltpu.SemaphoreType.DMA((COPIES,)),
            pltpu.SemaphoreType.DMA((COPIES,)),
            pltpu.SemaphoreType.DMA((3,)),
        ],
        compiler_params=pltpu.CompilerParams(
            collective_id=0, has_side_effects=True, vmem_limit_bytes=63 * 1024 * 1024
        ),
    )(tokens.reshape(TOK, width), grad_out.reshape(TOK, own_cols), weight)
    return grad_input.reshape(rows, cols, own_cols), grad_weight


def solution(mesh):
    placed = (P("lat", "lon", None), P("lat", "lon", "fsdp"), P(None, "fsdp", None))
    return jax.shard_map(
        shards,
        mesh=mesh,
        in_specs=placed,
        out_specs=(P("lat", "lon", "fsdp"), P(None, ("lat", "lon"), "fsdp")),
        check_vma=False,
    )
```

```python
import functools
import math

import jax
import jax.numpy as jnp
from jax import lax
from jax.experimental import pallas as pl
from jax.experimental.pallas import tpu as pltpu
from jax.sharding import PartitionSpec as P

HEADS = 16
RADIUS = 6
MESH = pl.DeviceIdType.MESH
BF16 = jnp.bfloat16
F32 = jnp.float32

ROWS, COLS = 8, 16
TOK = ROWS * COLS
BLOCKS = 6
EXT = BLOCKS * TOK
SLAB = RADIUS * ROWS
EAST, WEST = 0, 64
LATS, LONS, FSDP = 8, 16, 4
XS, YS, ZS = 4, 8, 8

NORTH_SOUTH, EAST_WEST, CORNERS = 0, 2, 4
GRADS = 8
WEIGHTS, SIDE_WEIGHTS, CORE_WEIGHTS = 16, 19, 25
STATS = 31
CORE_GRAD = 39
INPUT_SUMS = 42
SUM_X, SUM_LON = 45, 54
COPIES = 99


def dot(a, b, ca, cb, precision=None):
    return lax.dot_general(
        a, b, (((ca,), (cb,)), ((), ())), preferred_element_type=F32, precision=precision
    )


def place(block, spot):
    half = spot // 64
    inner = spot % 64
    side_col = inner // ROWS + jnp.where(half == 0, COLS, -RADIUS)
    is_tile = block < 3
    row = jnp.where(is_tile, spot // COLS, inner % ROWS)
    col = jnp.where(is_tile, spot % COLS, side_col)
    kind = block % 3
    shift = jnp.where(kind == 1, -ROWS, jnp.where(kind == 2, ROWS, 0))
    real = is_tile | (inner < SLAB)
    return row + shift, col, real


def bias_of(block, spot, own, lat):
    row, col, real = place(block, spot)
    own_row, own_col = own // COLS, own % COLS
    gap_r = row - own_row
    gap_c = col - own_col
    grid_row = lat * ROWS + row
    allowed = (
        real
        & (gap_r <= RADIUS)
        & (gap_r >= -RADIUS)
        & (gap_c <= RADIUS)
        & (gap_c >= -RADIUS)
        & (grid_row >= 0)
        & (grid_row < LATS * ROWS)
    )
    return jnp.where(allowed, 0.0, -jnp.inf).astype(F32)


def kernel(
    tokens,
    grad_out,
    weight,
    grad_input,
    grad_weight,
    xs,
    dos,
    packs,
    wbuf,
    qkv,
    bias_f,
    bias_b,
    stats,
    stats_in,
    stat_rows,
    grads,
    xt,
    scores_in,
    grad_probs,
    acc,
    gi_own,
    gi_out,
    gi_in,
    gx_out,
    gx_in,
    r1,
    gl_out,
    gl_in,
    send_sems,
    recv_sems,
    local_sems,
):
    lat = lax.axis_index("lat")
    lon = lax.axis_index("lon")
    fsdp = lax.axis_index("fsdp")
    x, core = lat // 2, lat % 2
    z_hi, y = lon // YS, lon % YS
    z = z_hi * FSDP + fsdp
    head_size = 64
    own_heads = HEADS // FSDP
    own_cols = own_heads * head_size
    width = FSDP * own_cols
    scale = 1.0 / math.sqrt(head_size)

    def at(*, d_lat=None, d_lon=None, d_fsdp=None):
        return (
            lat if d_lat is None else d_lat,
            lon if d_lon is None else d_lon,
            fsdp if d_fsdp is None else d_fsdp,
        )

    south_lat, north_lat = (lat + 1) % LATS, (lat + LATS - 1) % LATS
    east_lon, west_lon = (lon + 1) % LONS, (lon + LONS - 1) % LONS
    east_fsdp = jnp.where(y == YS - 1, FSDP - 1 - fsdp, fsdp)
    west_fsdp = jnp.where(y == 0, FSDP - 1 - fsdp, fsdp)
    south, north = at(d_lat=south_lat), at(d_lat=north_lat)
    east, west = at(d_lon=east_lon), at(d_lon=west_lon)
    east_copy = at(d_lon=east_lon, d_fsdp=east_fsdp)
    west_copy = at(d_lon=west_lon, d_fsdp=west_fsdp)
    other_core = at(d_lat=lat + 1 - 2 * core)

    def on_z(step):
        target = (z + step + ZS) % ZS
        return at(d_lon=(target // FSDP) * YS + y, d_fsdp=target % FSDP)

    def on_x(step):
        return at(d_lat=((x + step) % XS) * 2 + core)

    def on_y(step):
        return at(d_lon=z_hi * YS + (y + step) % YS)

    def on_lon(cross, step):
        half = 1 - z_hi if cross else z_hi
        return at(d_lon=half * YS + (y + step) % YS)

    corners = (
        at(d_lat=north_lat, d_lon=east_lon),
        at(d_lat=north_lat, d_lon=west_lon),
        at(d_lat=south_lat, d_lon=east_lon),
        at(d_lat=south_lat, d_lon=west_lon),
    )
    partners = [south, north, east, west, east_copy, west_copy, *corners]
    partners += [on_z(step) for step in (1, -1, 2, -2)]
    partners += [at(d_fsdp=(fsdp + step) % FSDP) for step in range(1, FSDP)]
    partners += [on_x(step) for step in range(1, XS)]
    lon_steps = [(1, step) for step in range(YS)] + [(0, step) for step in range(1, YS)]
    partners += [on_lon(*step) for step in lon_steps]

    barrier = pltpu.get_barrier_semaphore()
    for partner in partners:
        pl.semaphore_signal(barrier, inc=1, device_id=partner, device_id_type=MESH)

    own_tokens = pltpu.make_async_copy(tokens, xs.at[pl.ds(0, TOK)], local_sems.at[0])
    own_grads = pltpu.make_async_copy(grad_out, dos.at[pl.ds(0, TOK)], local_sems.at[1])
    own_start = pl.multiple_of(fsdp * own_cols, own_cols)
    own_weight = pltpu.make_async_copy(
        weight.at[:, :, pl.ds(own_start, own_cols)],
        wbuf.at[:, pl.ds(own_start, own_cols), :],
        local_sems.at[2],
    )
    own_tokens.start()
    own_grads.start()
    own_weight.start()

    def remote(src, dst, number, device):
        return pltpu.make_async_remote_copy(
            src_ref=src,
            dst_ref=dst,
            send_sem=send_sems.at[number],
            recv_sem=recv_sems.at[number],
            device_id=device,
            device_id_type=MESH,
        )

    pl.semaphore_wait(barrier, len(partners))

    sent = []

    def start(*args):
        copy = remote(*args)
        copy.start()
        sent.append(copy)
        return copy

    half_rows = own_cols // 2
    quarter = half_rows // 2
    eighth = quarter // 2
    parity = y % 2
    far = 2 - 4 * core
    mine_at = core * half_rows + parity * quarter
    other_at = core * half_rows + (1 - parity) * quarter

    def weight_rows(origin, offset, count):
        first = pl.multiple_of(origin * own_cols + offset, eighth)
        return wbuf.at[:, pl.ds(first, count), :]

    weight_copies = []
    for number, step in enumerate((1, -1, far)):
        target = on_z(step)
        cols = pl.multiple_of(target[2] * own_cols, own_cols)
        weight_copies.append(
            start(
                weight.at[
                    :, pl.ds(pl.multiple_of(mine_at, quarter), quarter), pl.ds(cols, own_cols)
                ],
                weight_rows(fsdp, mine_at, quarter),
                WEIGHTS + number,
                target,
            )
        )

    tile_copies = []
    for number, device, block in ((0, south, 1), (1, north, 2)):
        tile_copies.append(
            start(
                tokens, xs.at[pl.ds(block * TOK, TOK)], NORTH_SOUTH + number, device
            )
        )
    grad_tile_copies = []
    for number, device, block in ((0, south, 1), (1, north, 2)):
        grad_tile_copies.append(
            start(
                grad_out,
                dos.at[pl.ds(block * TOK, TOK)],
                GRADS + NORTH_SOUTH + number,
                device,
            )
        )

    own_tokens.wait()
    own_grads.wait()
    spot = lax.broadcasted_iota(jnp.int32, (TOK, TOK), 0)
    flat = lax.broadcasted_iota(jnp.int32, (TOK, TOK), 1)
    inner = spot % 64
    source = (inner % ROWS) * COLS + inner // ROWS + jnp.where(spot < 64, 0, COLS - RADIUS)
    picks = (inner < SLAB) & (flat == source)
    pick = jnp.where(picks, 1.0, 0.0).astype(F32)
    pick_16 = pick.astype(BF16)
    packs[:, pl.ds(0, width)] = dot(pick_16, xs[pl.ds(0, TOK), :], 1, 0).astype(BF16)
    packs[:, pl.ds(width, own_cols)] = dot(pick_16, dos[pl.ds(0, TOK), :], 1, 0).astype(BF16)
    side_copies = []
    side = 3 * TOK
    for number, spot_at, token_device in ((0, EAST, west_copy), (1, WEST, east_copy)):
        side_copies.append(
            start(
                packs.at[pl.ds(spot_at, SLAB), pl.ds(0, width)],
                xs.at[pl.ds(side + spot_at, SLAB)],
                EAST_WEST + number,
                token_device,
            )
        )
    xt[:, pl.ds(0, TOK)] = xs[pl.ds(0, TOK), :].T

    for block in range(3, BLOCKS):
        for spot_at in (EAST, WEST):
            unused = pl.ds(block * TOK + spot_at + SLAB, 64 - SLAB)
            xs[unused, :] = jnp.zeros((64 - SLAB, width), BF16)
            dos[unused, :] = jnp.zeros((64 - SLAB, own_cols), BF16)

    @pl.loop(0, BLOCKS)
    def _(block):
        first = pl.multiple_of(block * TOK, TOK)
        bias_f[pl.ds(first, TOK), :] = bias_of(block, spot, flat, lat)
        bias_b[:, pl.ds(first, TOK)] = bias_of(block, flat, spot, lat)

    side_weight_copies = []
    core_weight_copies = []
    origins = [(fsdp + step + FSDP) % FSDP for step in (-1, 1, -far)]
    for number, origin in enumerate(origins):
        weight_copies[number].wait_recv()
        for leg, step in enumerate((1, -1)):
            region = weight_rows(origin, mine_at + leg * eighth, eighth)
            side_weight_copies.append(
                start(region, region, SIDE_WEIGHTS + 2 * number + leg, on_y(step))
            )
        region = weight_rows(origin, mine_at, quarter)
        core_weight_copies.append(start(region, region, CORE_WEIGHTS + 2 * number, other_core))
    corner_copies = []
    for number, spot_at in ((0, EAST), (1, WEST)):
        side_copies[number].wait_recv()
        for leg, (device, block) in enumerate(((south, 4), (north, 5))):
            corner_copies.append(
                start(
                    xs.at[pl.ds(side + spot_at, SLAB)],
                    xs.at[pl.ds(block * TOK + spot_at, SLAB)],
                    CORNERS + 2 * number + leg,
                    device,
                )
            )
    grad_side_copies = []
    for number, spot_at, device in ((0, EAST, west), (1, WEST, east)):
        grad_side_copies.append(
            start(
                packs.at[pl.ds(spot_at, SLAB), pl.ds(width, own_cols)],
                dos.at[pl.ds(side + spot_at, SLAB)],
                GRADS + EAST_WEST + number,
                device,
            )
        )

    for copy in tile_copies:
        copy.wait_recv()
    pair_rows = pl.ds(pl.multiple_of((2 - core) * TOK, TOK), TOK)
    xt[:, pl.ds(TOK, TOK)] = xs[pair_rows, :].T
    for number, origin in enumerate(origins):
        for leg in range(2):
            side_weight_copies[2 * number + leg].wait_recv()
        region = weight_rows(origin, other_at, quarter)
        core_weight_copies.append(start(region, region, CORE_WEIGHTS + 2 * number + 1, other_core))
    own_weight.wait()
    for copy in core_weight_copies + corner_copies:
        copy.wait_recv()

    @pl.loop(0, EXT // 256)
    def _(step):
        rows = pl.ds(pl.multiple_of(step * 256, 256), 256)
        block = xs[rows, :]
        for number in range(3):
            qkv[number, rows, :] = dot(block, wbuf[number], 1, 0).astype(BF16)

    lane = lax.broadcasted_iota(jnp.int32, (TOK, own_cols), 1) // head_size
    own = pl.ds(0, TOK)

    stats[pl.ds(3 * own_heads, own_heads), :] = jnp.zeros((own_heads, TOK), F32)

    grad_corner_copies = []
    for number, spot_at in ((0, EAST), (1, WEST)):
        grad_side_copies[number].wait_recv()
        for leg, (device, block) in enumerate(((south, 4), (north, 5))):
            grad_corner_copies.append(
                start(
                    dos.at[pl.ds(side + spot_at, SLAB)],
                    dos.at[pl.ds(block * TOK + spot_at, SLAB)],
                    GRADS + CORNERS + 2 * number + leg,
                    device,
                )
            )

    @pl.loop(0, own_heads)
    def _(head):
        mine = lane == head
        query = jnp.where(mine, qkv[0, own, :], 0).astype(BF16)
        cotangent = jnp.where(mine, dos[own, :], 0).astype(BF16)
        scores = dot(qkv[1], query, 1, 1) * scale + bias_f[...]
        row_max = jnp.max(scores, axis=0, keepdims=True)
        prob = jnp.exp(scores - row_max)
        inv_sum = 1.0 / jnp.sum(prob, axis=0, keepdims=True)
        prob = prob * inv_sum
        grad_prob = dot(qkv[2], cotangent, 1, 1)
        delta = jnp.sum(prob * grad_prob, axis=0, keepdims=True)
        grad_score = (scale * (prob * (grad_prob - delta))).astype(BF16)
        part = dot(grad_score, qkv[1], 0, 0)
        acc[0] = jnp.where(mine, part, acc[0])
        stats[pl.ds(head, 1), :] = row_max
        stats[pl.ds(own_heads + head, 1), :] = inv_sum
        stats[pl.ds(2 * own_heads + head, 1), :] = delta

    stats[pl.ds(16, 16), :] = dot(
        stats[pl.ds(0, 16), :], pick, 1, 1, precision=lax.Precision.HIGHEST
    )
    tile_stats = stats.at[pl.ds(0, 16)]
    side_stats = stats.at[pl.ds(16, 16)]
    stat_copies = []
    for number, (src, device) in enumerate(
        (
            (tile_stats, south),
            (tile_stats, north),
            (side_stats, west),
            (side_stats, east),
            (side_stats, corners[3]),
            (side_stats, corners[2]),
            (side_stats, corners[1]),
            (side_stats, corners[0]),
        )
    ):
        stat_copies.append(start(src, stats_in.at[number], STATS + number, device))

    parts = tuple((number * own_cols, own_cols) for number in (0, 2, 1))
    core_copies = []
    x_copies = [[], [], []]
    lon_copies = [[], [], []]

    def share_with_core(part):
        cols = pl.ds(*parts[part])
        return start(
            grads.at[own, cols],
            grads.at[pl.ds(TOK, TOK), cols],
            CORE_GRAD + part,
            other_core,
        )

    def input_terms(owner, numbers):
        rows = pl.ds(pl.multiple_of(owner * own_cols, own_cols), own_cols)
        total = None
        for number in numbers:
            term = dot(
                grads[own, pl.ds(number * own_cols, own_cols)], wbuf[number, rows, :], 1, 1
            )
            total = term if total is None else total + term
        return total

    def send_x(part):
        core_copies[part].wait_recv()
        cols = pl.ds(*parts[part])

        def terms(owner):
            rows = pl.ds(pl.multiple_of(owner * TOK, TOK), TOK)
            return dot(xt[rows, :], grads[:, cols], 1, 0)

        for step in range(1, XS):
            gx_out[step - 1, :, cols] = terms(((x + step) % XS) * 2 + core).astype(BF16)
            x_copies[part].append(
                start(
                    gx_out.at[step - 1, :, cols],
                    gx_in.at[step - 1, :, cols],
                    SUM_X + (XS - 1) * part + step - 1,
                    on_x(step),
                )
            )
        r1[:, cols] = terms(lat)

    def send_lon(part):
        first, count = parts[part]
        half = count // 2
        cols = pl.ds(first, count)
        folded = pl.ds(first // 2, half)
        for copy in x_copies[part]:
            copy.wait_recv()
        total = r1[:, cols]
        for number in range(XS - 1):
            total = total + gx_in[number, :, cols].astype(F32)
        r1[:, cols] = total
        for number, step in enumerate(lon_steps):
            target = on_lon(*step)
            rows = pl.ds(pl.multiple_of(target[1] * 8, 8), 8)
            gl_out[number, :, folded] = jnp.concatenate(
                [r1[rows, pl.ds(first, half)], r1[rows, pl.ds(first + half, half)]], axis=0
            ).astype(BF16)
            lon_copies[part].append(
                start(
                    gl_out.at[number, :, folded],
                    gl_in.at[number, :, folded],
                    SUM_LON + len(lon_steps) * part + number,
                    target,
                )
            )

    def finish(part):
        first, count = parts[part]
        half = count // 2
        folded = pl.ds(first // 2, half)
        rows = pl.ds(pl.multiple_of(lon * 8, 8), 8)
        total = jnp.concatenate(
            [r1[rows, pl.ds(first, half)], r1[rows, pl.ds(first + half, half)]], axis=0
        )
        for number in reversed(range(len(lon_steps))):
            lon_copies[part][number].wait_recv()
            total = total + gl_in[number, :, folded].astype(F32)
        total = total * weight_scale
        grad_weight[first // own_cols, :, pl.ds(0, half)] = total[:8]
        grad_weight[first // own_cols, :, pl.ds(half, half)] = total[8:]

    weight_scale = 1.0 / math.sqrt(TOK * LATS * LONS)
    grads[own, pl.ds(0, own_cols)] = acc[0].astype(BF16)
    core_copies.append(share_with_core(0))

    for copy in grad_tile_copies + grad_corner_copies:
        copy.wait_recv()

    @pl.loop(0, own_heads)
    def _(head):
        mine = lane == head
        key = jnp.where(mine, qkv[1, own, :], 0).astype(BF16)
        value = jnp.where(mine, qkv[2, own, :], 0).astype(BF16)
        scores_in[head] = dot(key, qkv[0], 1, 1) * scale + bias_b[...]
        grad_probs[head] = dot(value, dos[...], 1, 1)

    for step in range(FSDP):
        gi_own[step] = input_terms((fsdp + step) % FSDP, (0,))
    send_x(0)
    for copy in stat_copies:
        copy.wait_recv()
    half_lane = lax.broadcasted_iota(jnp.int32, (16, TOK), 1) < 64
    stat_rows[:, pl.ds(0, TOK)] = stats[pl.ds(0, 16), :]
    stat_rows[:, pl.ds(TOK, TOK)] = stats_in[0]
    stat_rows[:, pl.ds(2 * TOK, TOK)] = stats_in[1]
    for block in range(3):
        first = 2 + 2 * block
        stat_rows[:, pl.ds((3 + block) * TOK, TOK)] = jnp.where(
            half_lane, stats_in[first], stats_in[first + 1]
        )

    @pl.loop(0, own_heads)
    def _(head):
        mine = lane == head
        row_max = stat_rows[pl.ds(head, 1), :]
        inv_sum = stat_rows[pl.ds(own_heads + head, 1), :]
        prob = jnp.exp(jnp.minimum(scores_in[head] - row_max, 0.0)) * inv_sum
        scores_in[head] = prob
        acc[2] = jnp.where(mine, dot(prob.astype(BF16), dos[...], 1, 0), acc[2])

    grads[own, pl.ds(2 * own_cols, own_cols)] = acc[2].astype(BF16)
    core_copies.append(share_with_core(1))

    @pl.loop(0, own_heads)
    def _(head):
        mine = lane == head
        delta = stat_rows[pl.ds(2 * own_heads + head, 1), :]
        grad_score = (scale * (scores_in[head] * (grad_probs[head] - delta))).astype(BF16)
        acc[1] = jnp.where(mine, dot(grad_score, qkv[0], 1, 0), acc[1])

    grads[own, pl.ds(own_cols, own_cols)] = acc[1].astype(BF16)
    core_copies.append(share_with_core(2))
    send_x(1)
    for step in range(FSDP):
        gi_own[step] = gi_own[step] + input_terms((fsdp + step) % FSDP, (2,))
    send_x(2)
    input_copies = []
    for step in range(1, FSDP):
        peer = (fsdp + step) % FSDP
        gi_out[step - 1] = (gi_own[step] + input_terms(peer, (1,))).astype(BF16)
        input_copies.append(
            start(gi_out.at[step - 1], gi_in.at[step - 1], INPUT_SUMS + step - 1, at(d_fsdp=peer))
        )
    gi_own[0] = gi_own[0] + input_terms(fsdp, (1,))
    send_lon(0)
    send_lon(1)
    send_lon(2)
    for copy in input_copies:
        copy.wait_recv()
    grad_input[...] = (
        gi_own[0] + gi_in[0].astype(F32) + gi_in[1].astype(F32) + gi_in[2].astype(F32)
    ).astype(BF16)
    finish(0)
    finish(1)
    finish(2)

    for copy in sent:
        copy.wait_send()


def shards(tokens, grad_out, weight):
    rows, cols, width = tokens.shape
    own_cols = grad_out.shape[2]
    three = weight.shape[0]
    anywhere = pl.BlockSpec(memory_space=pl.ANY)
    in_vmem = pl.BlockSpec(memory_space=pltpu.VMEM)
    total = three * own_cols
    grad_input, grad_weight = pl.pallas_call(
        kernel,
        out_shape=(
            jax.ShapeDtypeStruct((TOK, own_cols), BF16),
            jax.ShapeDtypeStruct((three, 8, own_cols), F32),
        ),
        in_specs=[anywhere] * 3,
        out_specs=(in_vmem, in_vmem),
        scratch_shapes=[
            pltpu.VMEM((EXT, width), BF16),
            pltpu.VMEM((EXT, own_cols), BF16),
            pltpu.VMEM((TOK, width + own_cols), BF16),
            pltpu.VMEM((three, width, own_cols), BF16),
            pltpu.VMEM((three, EXT, own_cols), BF16),
            pltpu.VMEM((EXT, TOK), F32),
            pltpu.VMEM((TOK, EXT), F32),
            pltpu.VMEM((32, TOK), F32),
            pltpu.VMEM((8, 16, TOK), F32),
            pltpu.VMEM((16, EXT), F32),
            pltpu.VMEM((2 * TOK, total), BF16),
            pltpu.VMEM((width, 2 * TOK), BF16),
            pltpu.VMEM((own_cols // 64, TOK, EXT), F32),
            pltpu.VMEM((own_cols // 64, TOK, EXT), F32),
            pltpu.VMEM((three, TOK, own_cols), F32),
            pltpu.VMEM((FSDP, TOK, own_cols), F32),
            pltpu.VMEM((FSDP - 1, TOK, own_cols), BF16),
            pltpu.VMEM((FSDP - 1, TOK, own_cols), BF16),
            pltpu.VMEM((XS - 1, TOK, total), BF16),
            pltpu.VMEM((XS - 1, TOK, total), BF16),
            pltpu.VMEM((TOK, total), F32),
            pltpu.VMEM((LONS - 1, 16, total // 2), BF16),
            pltpu.VMEM((LONS - 1, 16, total // 2), BF16),
            pltpu.SemaphoreType.DMA((COPIES,)),
            pltpu.SemaphoreType.DMA((COPIES,)),
            pltpu.SemaphoreType.DMA((3,)),
        ],
        compiler_params=pltpu.CompilerParams(
            collective_id=0, has_side_effects=True, vmem_limit_bytes=63 * 1024 * 1024
        ),
    )(tokens.reshape(TOK, width), grad_out.reshape(TOK, own_cols), weight)
    return grad_input.reshape(rows, cols, own_cols), grad_weight


def solution(mesh):
    placed = (P("lat", "lon", None), P("lat", "lon", "fsdp"), P(None, "fsdp", None))
    return jax.shard_map(
        shards,
        mesh=mesh,
        in_specs=placed,
        out_specs=(P("lat", "lon", "fsdp"), P(None, ("lat", "lon"), "fsdp")),
        check_vma=False,
    )
```

```python
import functools
import math

import jax
import jax.numpy as jnp
from jax import lax
from jax.experimental import pallas as pl
from jax.experimental.pallas import tpu as pltpu
from jax.sharding import PartitionSpec as P

HEADS = 16
RADIUS = 6
MESH = pl.DeviceIdType.MESH
BF16 = jnp.bfloat16
F32 = jnp.float32

ROWS, COLS = 8, 16
TOK = ROWS * COLS
BLOCKS = 6
EXT = BLOCKS * TOK
SLAB = RADIUS * ROWS
EAST, WEST = 0, 64
LATS, LONS, FSDP = 8, 16, 4
XS, YS, ZS = 4, 8, 8

NORTH_SOUTH, EAST_WEST, CORNERS = 0, 2, 4
GRADS = 8
WEIGHTS, SIDE_WEIGHTS, CORE_WEIGHTS = 16, 19, 25
STATS = 31
CORE_GRAD = 39
INPUT_SUMS = 42
SUM_X, SUM_LON = 45, 54
COPIES = 99


def dot(a, b, ca, cb, precision=None):
    return lax.dot_general(
        a, b, (((ca,), (cb,)), ((), ())), preferred_element_type=F32, precision=precision
    )


def place(block, spot):
    half = spot // 64
    inner = spot % 64
    side_col = inner // ROWS + jnp.where(half == 0, COLS, -RADIUS)
    is_tile = block < 3
    row = jnp.where(is_tile, spot // COLS, inner % ROWS)
    col = jnp.where(is_tile, spot % COLS, side_col)
    kind = block % 3
    shift = jnp.where(kind == 1, -ROWS, jnp.where(kind == 2, ROWS, 0))
    real = is_tile | (inner < SLAB)
    return row + shift, col, real


def bias_of(block, spot, own, lat):
    row, col, real = place(block, spot)
    own_row, own_col = own // COLS, own % COLS
    gap_r = row - own_row
    gap_c = col - own_col
    grid_row = lat * ROWS + row
    allowed = (
        real
        & (gap_r <= RADIUS)
        & (gap_r >= -RADIUS)
        & (gap_c <= RADIUS)
        & (gap_c >= -RADIUS)
        & (grid_row >= 0)
        & (grid_row < LATS * ROWS)
    )
    return jnp.where(allowed, 0.0, -jnp.inf).astype(F32)


def kernel(
    tokens,
    grad_out,
    weight,
    grad_input,
    grad_weight,
    xs,
    dos,
    packs,
    wbuf,
    qkv,
    bias_f,
    bias_b,
    stats,
    stats_in,
    stat_rows,
    grads,
    xt,
    probs,
    own_grad_probs,
    scores_in,
    grad_probs,
    acc,
    gi_own,
    gi_out,
    gi_in,
    gx_out,
    gx_in,
    r1,
    gl_out,
    gl_in,
    send_sems,
    recv_sems,
    local_sems,
):
    lat = lax.axis_index("lat")
    lon = lax.axis_index("lon")
    fsdp = lax.axis_index("fsdp")
    x, core = lat // 2, lat % 2
    z_hi, y = lon // YS, lon % YS
    z = z_hi * FSDP + fsdp
    head_size = 64
    own_heads = HEADS // FSDP
    own_cols = own_heads * head_size
    width = FSDP * own_cols
    scale = 1.0 / math.sqrt(head_size)

    def at(*, d_lat=None, d_lon=None, d_fsdp=None):
        return (
            lat if d_lat is None else d_lat,
            lon if d_lon is None else d_lon,
            fsdp if d_fsdp is None else d_fsdp,
        )

    south_lat, north_lat = (lat + 1) % LATS, (lat + LATS - 1) % LATS
    east_lon, west_lon = (lon + 1) % LONS, (lon + LONS - 1) % LONS
    east_fsdp = jnp.where(y == YS - 1, FSDP - 1 - fsdp, fsdp)
    west_fsdp = jnp.where(y == 0, FSDP - 1 - fsdp, fsdp)
    south, north = at(d_lat=south_lat), at(d_lat=north_lat)
    east, west = at(d_lon=east_lon), at(d_lon=west_lon)
    east_copy = at(d_lon=east_lon, d_fsdp=east_fsdp)
    west_copy = at(d_lon=west_lon, d_fsdp=west_fsdp)
    other_core = at(d_lat=lat + 1 - 2 * core)

    def on_z(step):
        target = (z + step + ZS) % ZS
        return at(d_lon=(target // FSDP) * YS + y, d_fsdp=target % FSDP)

    def on_x(step):
        return at(d_lat=((x + step) % XS) * 2 + core)

    def on_y(step):
        return at(d_lon=z_hi * YS + (y + step) % YS)

    def on_lon(cross, step):
        half = 1 - z_hi if cross else z_hi
        return at(d_lon=half * YS + (y + step) % YS)

    corners = (
        at(d_lat=north_lat, d_lon=east_lon),
        at(d_lat=north_lat, d_lon=west_lon),
        at(d_lat=south_lat, d_lon=east_lon),
        at(d_lat=south_lat, d_lon=west_lon),
    )
    partners = [*corners, east_copy, west_copy, south, north]
    partners += [on_z(step) for step in (1, -1, 2, -2)]
    partners += [at(d_fsdp=(fsdp + step) % FSDP) for step in range(1, FSDP)]
    partners += [on_x(step) for step in range(1, XS)]
    lon_steps = [(1, step) for step in range(YS)] + [(0, step) for step in range(1, YS)]
    partners += [on_lon(*step) for step in lon_steps]

    barrier = pltpu.get_barrier_semaphore()
    for partner in partners:
        pl.semaphore_signal(barrier, inc=1, device_id=partner, device_id_type=MESH)

    own_tokens = pltpu.make_async_copy(tokens, xs.at[pl.ds(0, TOK)], local_sems.at[0])
    own_grads = pltpu.make_async_copy(grad_out, dos.at[pl.ds(0, TOK)], local_sems.at[1])
    own_start = pl.multiple_of(fsdp * own_cols, own_cols)
    own_weight = pltpu.make_async_copy(
        weight.at[:, :, pl.ds(own_start, own_cols)],
        wbuf.at[:, pl.ds(own_start, own_cols), :],
        local_sems.at[2],
    )
    own_tokens.start()
    own_grads.start()
    own_weight.start()

    def remote(src, dst, number, device):
        return pltpu.make_async_remote_copy(
            src_ref=src,
            dst_ref=dst,
            send_sem=send_sems.at[number],
            recv_sem=recv_sems.at[number],
            device_id=device,
            device_id_type=MESH,
        )

    pl.semaphore_wait(barrier, len(partners))

    sent = []

    def start(*args):
        copy = remote(*args)
        copy.start()
        sent.append(copy)
        return copy

    half_rows = own_cols // 2
    quarter = half_rows // 2
    eighth = quarter // 2
    parity = y % 2
    far = 2 - 4 * core
    mine_at = core * half_rows + parity * quarter
    other_at = core * half_rows + (1 - parity) * quarter

    def weight_rows(origin, offset, count):
        first = pl.multiple_of(origin * own_cols + offset, eighth)
        return wbuf.at[:, pl.ds(first, count), :]

    weight_copies = []
    for number, step in enumerate((1, -1, far)):
        target = on_z(step)
        cols = pl.multiple_of(target[2] * own_cols, own_cols)
        weight_copies.append(
            start(
                weight.at[
                    :, pl.ds(pl.multiple_of(mine_at, quarter), quarter), pl.ds(cols, own_cols)
                ],
                weight_rows(fsdp, mine_at, quarter),
                WEIGHTS + number,
                target,
            )
        )

    tile_copies = []
    for number, device, block in ((0, south, 1), (1, north, 2)):
        tile_copies.append(
            start(
                tokens, xs.at[pl.ds(block * TOK, TOK)], NORTH_SOUTH + number, device
            )
        )
    grad_tile_copies = []
    for number, device, block in ((0, south, 1), (1, north, 2)):
        grad_tile_copies.append(
            start(
                grad_out,
                dos.at[pl.ds(block * TOK, TOK)],
                GRADS + NORTH_SOUTH + number,
                device,
            )
        )

    own_tokens.wait()
    own_grads.wait()
    spot = lax.broadcasted_iota(jnp.int32, (TOK, TOK), 0)
    flat = lax.broadcasted_iota(jnp.int32, (TOK, TOK), 1)
    inner = spot % 64
    source = (inner % ROWS) * COLS + inner // ROWS + jnp.where(spot < 64, 0, COLS - RADIUS)
    picks = (inner < SLAB) & (flat == source)
    pick = jnp.where(picks, 1.0, 0.0).astype(F32)
    pick_16 = pick.astype(BF16)
    packs[:, pl.ds(0, width)] = dot(pick_16, xs[pl.ds(0, TOK), :], 1, 0).astype(BF16)
    packs[:, pl.ds(width, own_cols)] = dot(pick_16, dos[pl.ds(0, TOK), :], 1, 0).astype(BF16)
    side_copies = []
    side = 3 * TOK
    for number, spot_at, token_device in ((0, EAST, west_copy), (1, WEST, east_copy)):
        side_copies.append(
            start(
                packs.at[pl.ds(spot_at, SLAB), pl.ds(0, width)],
                xs.at[pl.ds(side + spot_at, SLAB)],
                EAST_WEST + number,
                token_device,
            )
        )
    xt[:, pl.ds(0, TOK)] = xs[pl.ds(0, TOK), :].T

    for block in range(3, BLOCKS):
        for spot_at in (EAST, WEST):
            unused = pl.ds(block * TOK + spot_at + SLAB, 64 - SLAB)
            xs[unused, :] = jnp.zeros((64 - SLAB, width), BF16)
            dos[unused, :] = jnp.zeros((64 - SLAB, own_cols), BF16)

    @pl.loop(0, BLOCKS)
    def _(block):
        first = pl.multiple_of(block * TOK, TOK)
        bias_f[pl.ds(first, TOK), :] = bias_of(block, spot, flat, lat)
        bias_b[:, pl.ds(first, TOK)] = bias_of(block, flat, spot, lat)

    side_weight_copies = []
    core_weight_copies = []
    origins = [(fsdp + step + FSDP) % FSDP for step in (-1, 1, -far)]
    for number, origin in enumerate(origins):
        weight_copies[number].wait_recv()
        for leg, step in enumerate((1, -1)):
            region = weight_rows(origin, mine_at + leg * eighth, eighth)
            side_weight_copies.append(
                start(region, region, SIDE_WEIGHTS + 2 * number + leg, on_y(step))
            )
        region = weight_rows(origin, mine_at, quarter)
        core_weight_copies.append(start(region, region, CORE_WEIGHTS + 2 * number, other_core))
    corner_copies = []
    for number, spot_at in ((0, EAST), (1, WEST)):
        side_copies[number].wait_recv()
        for leg, (device, block) in enumerate(((south, 4), (north, 5))):
            corner_copies.append(
                start(
                    xs.at[pl.ds(side + spot_at, SLAB)],
                    xs.at[pl.ds(block * TOK + spot_at, SLAB)],
                    CORNERS + 2 * number + leg,
                    device,
                )
            )
    grad_side_copies = []
    for number, spot_at, device in ((0, EAST, west), (1, WEST, east)):
        grad_side_copies.append(
            start(
                packs.at[pl.ds(spot_at, SLAB), pl.ds(width, own_cols)],
                dos.at[pl.ds(side + spot_at, SLAB)],
                GRADS + EAST_WEST + number,
                device,
            )
        )

    for copy in tile_copies:
        copy.wait_recv()
    pair_rows = pl.ds(pl.multiple_of((2 - core) * TOK, TOK), TOK)
    xt[:, pl.ds(TOK, TOK)] = xs[pair_rows, :].T
    for number, origin in enumerate(origins):
        for leg in range(2):
            side_weight_copies[2 * number + leg].wait_recv()
        region = weight_rows(origin, other_at, quarter)
        core_weight_copies.append(start(region, region, CORE_WEIGHTS + 2 * number + 1, other_core))
    own_weight.wait()
    for copy in core_weight_copies + corner_copies:
        copy.wait_recv()

    @pl.loop(0, EXT // 256)
    def _(step):
        rows = pl.ds(pl.multiple_of(step * 256, 256), 256)
        block = xs[rows, :]
        for number in range(3):
            qkv[number, rows, :] = dot(block, wbuf[number], 1, 0).astype(BF16)

    lane = lax.broadcasted_iota(jnp.int32, (TOK, own_cols), 1) // head_size
    own = pl.ds(0, TOK)

    stats[pl.ds(3 * own_heads, own_heads), :] = jnp.zeros((own_heads, TOK), F32)

    @pl.loop(0, own_heads, unroll=True)
    def _(head):
        mine = lane == head
        query = jnp.where(mine, qkv[0, own, :], 0).astype(BF16)
        cotangent = jnp.where(mine, dos[own, :], 0).astype(BF16)
        scores = dot(qkv[1], query, 1, 1) * scale + bias_f[...]
        row_max = jnp.max(scores, axis=0, keepdims=True)
        prob = jnp.exp(scores - row_max)
        inv_sum = 1.0 / jnp.sum(prob, axis=0, keepdims=True)
        prob = prob * inv_sum
        grad_prob = dot(qkv[2], cotangent, 1, 1)
        delta = jnp.sum(prob * grad_prob, axis=0, keepdims=True)
        probs[head] = prob
        own_grad_probs[head] = grad_prob
        stats[pl.ds(head, 1), :] = row_max
        stats[pl.ds(own_heads + head, 1), :] = inv_sum
        stats[pl.ds(2 * own_heads + head, 1), :] = delta

    stats[pl.ds(16, 16), :] = dot(
        stats[pl.ds(0, 16), :], pick, 1, 1, precision=lax.Precision.HIGHEST
    )
    tile_stats = stats.at[pl.ds(0, 16)]
    side_stats = stats.at[pl.ds(16, 16)]
    stat_copies = []
    for number, (src, device) in enumerate(
        (
            (tile_stats, south),
            (tile_stats, north),
            (side_stats, west),
            (side_stats, east),
            (side_stats, corners[3]),
            (side_stats, corners[2]),
            (side_stats, corners[1]),
            (side_stats, corners[0]),
        )
    ):
        stat_copies.append(start(src, stats_in.at[number], STATS + number, device))

    grad_corner_copies = []
    for number, spot_at in ((0, EAST), (1, WEST)):
        grad_side_copies[number].wait_recv()
        for leg, (device, block) in enumerate(((south, 4), (north, 5))):
            grad_corner_copies.append(
                start(
                    dos.at[pl.ds(side + spot_at, SLAB)],
                    dos.at[pl.ds(block * TOK + spot_at, SLAB)],
                    GRADS + CORNERS + 2 * number + leg,
                    device,
                )
            )

    parts = tuple((number * own_cols, own_cols) for number in (0, 2, 1))
    core_copies = []
    x_copies = [[], [], []]
    lon_copies = [[], [], []]

    def share_with_core(part):
        cols = pl.ds(*parts[part])
        return start(
            grads.at[own, cols],
            grads.at[pl.ds(TOK, TOK), cols],
            CORE_GRAD + part,
            other_core,
        )

    def input_terms(owner, numbers):
        rows = pl.ds(pl.multiple_of(owner * own_cols, own_cols), own_cols)
        total = None
        for number in numbers:
            term = dot(
                grads[own, pl.ds(number * own_cols, own_cols)], wbuf[number, rows, :], 1, 1
            )
            total = term if total is None else total + term
        return total

    def send_x(part):
        core_copies[part].wait_recv()
        cols = pl.ds(*parts[part])

        def terms(owner):
            rows = pl.ds(pl.multiple_of(owner * TOK, TOK), TOK)
            return dot(xt[rows, :], grads[:, cols], 1, 0)

        for step in range(1, XS):
            gx_out[step - 1, :, cols] = terms(((x + step) % XS) * 2 + core).astype(BF16)
            x_copies[part].append(
                start(
                    gx_out.at[step - 1, :, cols],
                    gx_in.at[step - 1, :, cols],
                    SUM_X + (XS - 1) * part + step - 1,
                    on_x(step),
                )
            )
        r1[:, cols] = terms(lat)

    def send_lon(part):
        first, count = parts[part]
        half = count // 2
        cols = pl.ds(first, count)
        folded = pl.ds(first // 2, half)
        for copy in x_copies[part]:
            copy.wait_recv()
        total = r1[:, cols]
        for number in range(XS - 1):
            total = total + gx_in[number, :, cols].astype(F32)
        r1[:, cols] = total
        for number, step in enumerate(lon_steps):
            target = on_lon(*step)
            rows = pl.ds(pl.multiple_of(target[1] * 8, 8), 8)
            gl_out[number, :, folded] = jnp.concatenate(
                [r1[rows, pl.ds(first, half)], r1[rows, pl.ds(first + half, half)]], axis=0
            ).astype(BF16)
            lon_copies[part].append(
                start(
                    gl_out.at[number, :, folded],
                    gl_in.at[number, :, folded],
                    SUM_LON + len(lon_steps) * part + number,
                    target,
                )
            )

    def finish(part):
        first, count = parts[part]
        half = count // 2
        folded = pl.ds(first // 2, half)
        rows = pl.ds(pl.multiple_of(lon * 8, 8), 8)
        total = jnp.concatenate(
            [r1[rows, pl.ds(first, half)], r1[rows, pl.ds(first + half, half)]], axis=0
        )
        for number in reversed(range(len(lon_steps))):
            lon_copies[part][number].wait_recv()
            total = total + gl_in[number, :, folded].astype(F32)
        total = total * weight_scale
        grad_weight[first // own_cols, :, pl.ds(0, half)] = total[:8]
        grad_weight[first // own_cols, :, pl.ds(half, half)] = total[8:]

    @pl.loop(0, own_heads, unroll=True)
    def _(head):
        mine = lane == head
        delta = stats[pl.ds(2 * own_heads + head, 1), :]
        grad_score = (scale * (probs[head] * (own_grad_probs[head] - delta))).astype(BF16)
        acc[0] = jnp.where(mine, dot(grad_score, qkv[1], 0, 0), acc[0])

    weight_scale = 1.0 / math.sqrt(TOK * LATS * LONS)
    grads[own, pl.ds(0, own_cols)] = acc[0].astype(BF16)
    core_copies.append(share_with_core(0))

    for step in range(FSDP):
        gi_own[step] = input_terms((fsdp + step) % FSDP, (0,))
    send_x(0)
    for copy in grad_tile_copies + grad_corner_copies:
        copy.wait_recv()

    @pl.loop(0, own_heads, unroll=True)
    def _(head):
        mine = lane == head
        key = jnp.where(mine, qkv[1, own, :], 0).astype(BF16)
        value = jnp.where(mine, qkv[2, own, :], 0).astype(BF16)
        scores_in[head] = dot(key, qkv[0], 1, 1) * scale + bias_b[...]
        grad_probs[head] = dot(value, dos[...], 1, 1)

    for copy in stat_copies:
        copy.wait_recv()
    half_lane = lax.broadcasted_iota(jnp.int32, (16, TOK), 1) < 64
    stat_rows[:, pl.ds(0, TOK)] = stats[pl.ds(0, 16), :]
    stat_rows[:, pl.ds(TOK, TOK)] = stats_in[0]
    stat_rows[:, pl.ds(2 * TOK, TOK)] = stats_in[1]
    for block in range(3):
        first = 2 + 2 * block
        stat_rows[:, pl.ds((3 + block) * TOK, TOK)] = jnp.where(
            half_lane, stats_in[first], stats_in[first + 1]
        )

    @pl.loop(0, own_heads, unroll=True)
    def _(head):
        mine = lane == head
        row_max = stat_rows[pl.ds(head, 1), :]
        inv_sum = stat_rows[pl.ds(own_heads + head, 1), :]
        prob = jnp.exp(jnp.minimum(scores_in[head] - row_max, 0.0)) * inv_sum
        scores_in[head] = prob
        acc[2] = jnp.where(mine, dot(prob.astype(BF16), dos[...], 1, 0), acc[2])

    grads[own, pl.ds(2 * own_cols, own_cols)] = acc[2].astype(BF16)
    core_copies.append(share_with_core(1))

    @pl.loop(0, own_heads, unroll=True)
    def _(head):
        mine = lane == head
        delta = stat_rows[pl.ds(2 * own_heads + head, 1), :]
        grad_score = (scale * (scores_in[head] * (grad_probs[head] - delta))).astype(BF16)
        acc[1] = jnp.where(mine, dot(grad_score, qkv[0], 1, 0), acc[1])

    grads[own, pl.ds(own_cols, own_cols)] = acc[1].astype(BF16)
    core_copies.append(share_with_core(2))
    send_x(1)
    for step in range(FSDP):
        gi_own[step] = gi_own[step] + input_terms((fsdp + step) % FSDP, (2,))
    send_x(2)
    input_copies = []
    for step in range(1, FSDP):
        peer = (fsdp + step) % FSDP
        gi_out[step - 1] = (gi_own[step] + input_terms(peer, (1,))).astype(BF16)
        input_copies.append(
            start(gi_out.at[step - 1], gi_in.at[step - 1], INPUT_SUMS + step - 1, at(d_fsdp=peer))
        )
    gi_own[0] = gi_own[0] + input_terms(fsdp, (1,))
    send_lon(0)
    send_lon(1)
    finish(0)
    send_lon(2)
    for copy in input_copies:
        copy.wait_recv()
    grad_input[...] = (
        gi_own[0] + gi_in[0].astype(F32) + gi_in[1].astype(F32) + gi_in[2].astype(F32)
    ).astype(BF16)
    finish(1)
    finish(2)

    for copy in sent:
        copy.wait_send()


def shards(tokens, grad_out, weight):
    rows, cols, width = tokens.shape
    own_cols = grad_out.shape[2]
    three = weight.shape[0]
    anywhere = pl.BlockSpec(memory_space=pl.ANY)
    in_vmem = pl.BlockSpec(memory_space=pltpu.VMEM)
    total = three * own_cols
    grad_input, grad_weight = pl.pallas_call(
        kernel,
        out_shape=(
            jax.ShapeDtypeStruct((TOK, own_cols), BF16),
            jax.ShapeDtypeStruct((three, 8, own_cols), F32),
        ),
        in_specs=[anywhere] * 3,
        out_specs=(in_vmem, in_vmem),
        scratch_shapes=[
            pltpu.VMEM((EXT, width), BF16),
            pltpu.VMEM((EXT, own_cols), BF16),
            pltpu.VMEM((TOK, width + own_cols), BF16),
            pltpu.VMEM((three, width, own_cols), BF16),
            pltpu.VMEM((three, EXT, own_cols), BF16),
            pltpu.VMEM((EXT, TOK), F32),
            pltpu.VMEM((TOK, EXT), F32),
            pltpu.VMEM((32, TOK), F32),
            pltpu.VMEM((8, 16, TOK), F32),
            pltpu.VMEM((16, EXT), F32),
            pltpu.VMEM((2 * TOK, total), BF16),
            pltpu.VMEM((width, 2 * TOK), BF16),
            pltpu.VMEM((own_cols // 64, EXT, TOK), F32),
            pltpu.VMEM((own_cols // 64, EXT, TOK), F32),
            pltpu.VMEM((own_cols // 64, TOK, EXT), F32),
            pltpu.VMEM((own_cols // 64, TOK, EXT), F32),
            pltpu.VMEM((three, TOK, own_cols), F32),
            pltpu.VMEM((FSDP, TOK, own_cols), F32),
            pltpu.VMEM((FSDP - 1, TOK, own_cols), BF16),
            pltpu.VMEM((FSDP - 1, TOK, own_cols), BF16),
            pltpu.VMEM((XS - 1, TOK, total), BF16),
            pltpu.VMEM((XS - 1, TOK, total), BF16),
            pltpu.VMEM((TOK, total), F32),
            pltpu.VMEM((LONS - 1, 16, total // 2), BF16),
            pltpu.VMEM((LONS - 1, 16, total // 2), BF16),
            pltpu.SemaphoreType.DMA((COPIES,)),
            pltpu.SemaphoreType.DMA((COPIES,)),
            pltpu.SemaphoreType.DMA((3,)),
        ],
        compiler_params=pltpu.CompilerParams(
            collective_id=0, has_side_effects=True, vmem_limit_bytes=63 * 1024 * 1024
        ),
    )(tokens.reshape(TOK, width), grad_out.reshape(TOK, own_cols), weight)
    return grad_input.reshape(rows, cols, own_cols), grad_weight


def solution(mesh):
    placed = (P("lat", "lon", None), P("lat", "lon", "fsdp"), P(None, "fsdp", None))
    return jax.shard_map(
        shards,
        mesh=mesh,
        in_specs=placed,
        out_specs=(P("lat", "lon", "fsdp"), P(None, ("lat", "lon"), "fsdp")),
        check_vma=False,
    )
```

```python
import functools
import math

import jax
import jax.numpy as jnp
from jax import lax
from jax.experimental import pallas as pl
from jax.experimental.pallas import tpu as pltpu
from jax.sharding import PartitionSpec as P

HEADS = 16
RADIUS = 6
MESH = pl.DeviceIdType.MESH
BF16 = jnp.bfloat16
F32 = jnp.float32

ROWS, COLS = 8, 16
TOK = ROWS * COLS
BLOCKS = 6
EXT = BLOCKS * TOK
SLAB = RADIUS * ROWS
EAST, WEST = 0, 64
LATS, LONS, FSDP = 8, 16, 4
XS, YS, ZS = 4, 8, 8

NORTH_SOUTH, EAST_WEST, CORNERS = 0, 2, 4
GRADS = 8
WEIGHTS, SIDE_WEIGHTS, CORE_WEIGHTS = 16, 19, 25
STATS = 31
CORE_GRAD = 39
INPUT_SUMS = 42
SUM_X, SUM_LON = 45, 54
COPIES = 84


def dot(a, b, ca, cb, precision=None):
    return lax.dot_general(
        a, b, (((ca,), (cb,)), ((), ())), preferred_element_type=F32, precision=precision
    )


def place(block, spot):
    half = spot // 64
    inner = spot % 64
    side_col = inner // ROWS + jnp.where(half == 0, COLS, -RADIUS)
    is_tile = block < 3
    row = jnp.where(is_tile, spot // COLS, inner % ROWS)
    col = jnp.where(is_tile, spot % COLS, side_col)
    kind = block % 3
    shift = jnp.where(kind == 1, -ROWS, jnp.where(kind == 2, ROWS, 0))
    real = is_tile | (inner < SLAB)
    return row + shift, col, real


def bias_of(block, spot, own, lat):
    row, col, real = place(block, spot)
    own_row, own_col = own // COLS, own % COLS
    gap_r = row - own_row
    gap_c = col - own_col
    grid_row = lat * ROWS + row
    allowed = (
        real
        & (gap_r <= RADIUS)
        & (gap_r >= -RADIUS)
        & (gap_c <= RADIUS)
        & (gap_c >= -RADIUS)
        & (grid_row >= 0)
        & (grid_row < LATS * ROWS)
    )
    return jnp.where(allowed, 0.0, -jnp.inf).astype(F32)


def kernel(
    tokens,
    grad_out,
    weight,
    grad_input,
    grad_weight,
    xs,
    dos,
    packs,
    wbuf,
    qkv,
    bias_f,
    bias_b,
    stats,
    stats_in,
    stat_rows,
    grads,
    xt,
    probs,
    own_grad_probs,
    scores_in,
    grad_probs,
    acc,
    gi_own,
    gi_out,
    gi_in,
    gx_out,
    gx_in,
    r1,
    gl_out,
    gl_in,
    send_sems,
    recv_sems,
    local_sems,
):
    lat = lax.axis_index("lat")
    lon = lax.axis_index("lon")
    fsdp = lax.axis_index("fsdp")
    x, core = lat // 2, lat % 2
    z_hi, y = lon // YS, lon % YS
    z = z_hi * FSDP + fsdp
    head_size = 64
    own_heads = HEADS // FSDP
    own_cols = own_heads * head_size
    width = FSDP * own_cols
    scale = 1.0 / math.sqrt(head_size)

    def at(*, d_lat=None, d_lon=None, d_fsdp=None):
        return (
            lat if d_lat is None else d_lat,
            lon if d_lon is None else d_lon,
            fsdp if d_fsdp is None else d_fsdp,
        )

    south_lat, north_lat = (lat + 1) % LATS, (lat + LATS - 1) % LATS
    east_lon, west_lon = (lon + 1) % LONS, (lon + LONS - 1) % LONS
    east_fsdp = jnp.where(y == YS - 1, FSDP - 1 - fsdp, fsdp)
    west_fsdp = jnp.where(y == 0, FSDP - 1 - fsdp, fsdp)
    south, north = at(d_lat=south_lat), at(d_lat=north_lat)
    east, west = at(d_lon=east_lon), at(d_lon=west_lon)
    east_copy = at(d_lon=east_lon, d_fsdp=east_fsdp)
    west_copy = at(d_lon=west_lon, d_fsdp=west_fsdp)
    other_core = at(d_lat=lat + 1 - 2 * core)

    def on_z(step):
        target = (z + step + ZS) % ZS
        return at(d_lon=(target // FSDP) * YS + y, d_fsdp=target % FSDP)

    def on_x(step):
        return at(d_lat=((x + step) % XS) * 2 + core)

    def on_y(step):
        return at(d_lon=z_hi * YS + (y + step) % YS)

    def on_lon(cross, step):
        half = 1 - z_hi if cross else z_hi
        return at(d_lon=half * YS + (y + step) % YS)

    corners = (
        at(d_lat=north_lat, d_lon=east_lon),
        at(d_lat=north_lat, d_lon=west_lon),
        at(d_lat=south_lat, d_lon=east_lon),
        at(d_lat=south_lat, d_lon=west_lon),
    )
    partners = [*corners, east_copy, west_copy, south, north]
    partners += [on_z(step) for step in (1, -1, 2, -2)]
    partners += [at(d_fsdp=(fsdp + step) % FSDP) for step in range(1, FSDP)]
    partners += [on_x(step) for step in range(1, XS)]
    lon_steps = [(1, step) for step in range(YS)] + [(0, step) for step in range(1, YS)]
    partners += [on_lon(*step) for step in lon_steps]

    barrier = pltpu.get_barrier_semaphore()
    for partner in partners:
        pl.semaphore_signal(barrier, inc=1, device_id=partner, device_id_type=MESH)

    own_tokens = pltpu.make_async_copy(tokens, xs.at[pl.ds(0, TOK)], local_sems.at[0])
    own_grads = pltpu.make_async_copy(grad_out, dos.at[pl.ds(0, TOK)], local_sems.at[1])
    own_start = pl.multiple_of(fsdp * own_cols, own_cols)
    own_weight = pltpu.make_async_copy(
        weight.at[:, :, pl.ds(own_start, own_cols)],
        wbuf.at[:, pl.ds(own_start, own_cols), :],
        local_sems.at[2],
    )
    own_tokens.start()
    own_grads.start()
    own_weight.start()

    def remote(src, dst, number, device):
        return pltpu.make_async_remote_copy(
            src_ref=src,
            dst_ref=dst,
            send_sem=send_sems.at[number],
            recv_sem=recv_sems.at[number],
            device_id=device,
            device_id_type=MESH,
        )

    pl.semaphore_wait(barrier, len(partners))

    sent = []

    def start(*args):
        copy = remote(*args)
        copy.start()
        sent.append(copy)
        return copy

    half_rows = own_cols // 2
    quarter = half_rows // 2
    eighth = quarter // 2
    parity = y % 2
    far = 2 - 4 * core
    mine_at = core * half_rows + parity * quarter
    other_at = core * half_rows + (1 - parity) * quarter

    def weight_rows(origin, offset, count):
        first = pl.multiple_of(origin * own_cols + offset, eighth)
        return wbuf.at[:, pl.ds(first, count), :]

    weight_copies = []
    for number, step in enumerate((1, -1, far)):
        target = on_z(step)
        cols = pl.multiple_of(target[2] * own_cols, own_cols)
        weight_copies.append(
            start(
                weight.at[
                    :, pl.ds(pl.multiple_of(mine_at, quarter), quarter), pl.ds(cols, own_cols)
                ],
                weight_rows(fsdp, mine_at, quarter),
                WEIGHTS + number,
                target,
            )
        )

    tile_copies = []
    for number, device, block in ((0, south, 1), (1, north, 2)):
        tile_copies.append(
            start(
                tokens, xs.at[pl.ds(block * TOK, TOK)], NORTH_SOUTH + number, device
            )
        )
    grad_tile_copies = []
    for number, device, block in ((0, south, 1), (1, north, 2)):
        grad_tile_copies.append(
            start(
                grad_out,
                dos.at[pl.ds(block * TOK, TOK)],
                GRADS + NORTH_SOUTH + number,
                device,
            )
        )

    own_tokens.wait()
    own_grads.wait()
    spot = lax.broadcasted_iota(jnp.int32, (TOK, TOK), 0)
    flat = lax.broadcasted_iota(jnp.int32, (TOK, TOK), 1)
    inner = spot % 64
    source = (inner % ROWS) * COLS + inner // ROWS + jnp.where(spot < 64, 0, COLS - RADIUS)
    picks = (inner < SLAB) & (flat == source)
    pick = jnp.where(picks, 1.0, 0.0).astype(F32)
    pick_16 = pick.astype(BF16)
    packs[:, pl.ds(0, width)] = dot(pick_16, xs[pl.ds(0, TOK), :], 1, 0).astype(BF16)
    packs[:, pl.ds(width, own_cols)] = dot(pick_16, dos[pl.ds(0, TOK), :], 1, 0).astype(BF16)
    side_copies = []
    side = 3 * TOK
    for number, spot_at, token_device in ((0, EAST, west_copy), (1, WEST, east_copy)):
        side_copies.append(
            start(
                packs.at[pl.ds(spot_at, SLAB), pl.ds(0, width)],
                xs.at[pl.ds(side + spot_at, SLAB)],
                EAST_WEST + number,
                token_device,
            )
        )
    xt[:, pl.ds(0, TOK)] = xs[pl.ds(0, TOK), :].T

    for block in range(3, BLOCKS):
        for spot_at in (EAST, WEST):
            unused = pl.ds(block * TOK + spot_at + SLAB, 64 - SLAB)
            xs[unused, :] = jnp.zeros((64 - SLAB, width), BF16)
            dos[unused, :] = jnp.zeros((64 - SLAB, own_cols), BF16)

    @pl.loop(0, BLOCKS)
    def _(block):
        first = pl.multiple_of(block * TOK, TOK)
        bias_f[pl.ds(first, TOK), :] = bias_of(block, spot, flat, lat)
        bias_b[:, pl.ds(first, TOK)] = bias_of(block, flat, spot, lat)

    side_weight_copies = []
    core_weight_copies = []
    origins = [(fsdp + step + FSDP) % FSDP for step in (-1, 1, -far)]
    for number, origin in enumerate(origins):
        weight_copies[number].wait_recv()
        for leg, step in enumerate((1, -1)):
            region = weight_rows(origin, mine_at + leg * eighth, eighth)
            side_weight_copies.append(
                start(region, region, SIDE_WEIGHTS + 2 * number + leg, on_y(step))
            )
        region = weight_rows(origin, mine_at, quarter)
        core_weight_copies.append(start(region, region, CORE_WEIGHTS + 2 * number, other_core))
    corner_copies = []
    for number, spot_at in ((0, EAST), (1, WEST)):
        side_copies[number].wait_recv()
        for leg, (device, block) in enumerate(((south, 4), (north, 5))):
            corner_copies.append(
                start(
                    xs.at[pl.ds(side + spot_at, SLAB)],
                    xs.at[pl.ds(block * TOK + spot_at, SLAB)],
                    CORNERS + 2 * number + leg,
                    device,
                )
            )
    grad_side_copies = []
    for number, spot_at, device in ((0, EAST, west), (1, WEST, east)):
        grad_side_copies.append(
            start(
                packs.at[pl.ds(spot_at, SLAB), pl.ds(width, own_cols)],
                dos.at[pl.ds(side + spot_at, SLAB)],
                GRADS + EAST_WEST + number,
                device,
            )
        )

    for copy in tile_copies:
        copy.wait_recv()
    pair_rows = pl.ds(pl.multiple_of((2 - core) * TOK, TOK), TOK)
    xt[:, pl.ds(TOK, TOK)] = xs[pair_rows, :].T
    for number, origin in enumerate(origins):
        for leg in range(2):
            side_weight_copies[2 * number + leg].wait_recv()
        region = weight_rows(origin, other_at, quarter)
        core_weight_copies.append(start(region, region, CORE_WEIGHTS + 2 * number + 1, other_core))
    own_weight.wait()
    for copy in core_weight_copies + corner_copies:
        copy.wait_recv()

    @pl.loop(0, EXT // 256)
    def _(step):
        rows = pl.ds(pl.multiple_of(step * 256, 256), 256)
        block = xs[rows, :]
        for number in range(3):
            qkv[number, rows, :] = dot(block, wbuf[number], 1, 0).astype(BF16)

    lane = lax.broadcasted_iota(jnp.int32, (TOK, own_cols), 1) // head_size
    own = pl.ds(0, TOK)

    stats[pl.ds(3 * own_heads, own_heads), :] = jnp.zeros((own_heads, TOK), F32)

    @pl.loop(0, own_heads, unroll=True)
    def _(head):
        mine = lane == head
        query = jnp.where(mine, qkv[0, own, :], 0).astype(BF16)
        cotangent = jnp.where(mine, dos[own, :], 0).astype(BF16)
        scores = dot(qkv[1], query, 1, 1) * scale + bias_f[...]
        row_max = jnp.max(scores, axis=0, keepdims=True)
        prob = jnp.exp(scores - row_max)
        inv_sum = 1.0 / jnp.sum(prob, axis=0, keepdims=True)
        prob = prob * inv_sum
        grad_prob = dot(qkv[2], cotangent, 1, 1)
        delta = jnp.sum(prob * grad_prob, axis=0, keepdims=True)
        probs[head] = prob
        own_grad_probs[head] = grad_prob
        stats[pl.ds(head, 1), :] = row_max
        stats[pl.ds(own_heads + head, 1), :] = inv_sum
        stats[pl.ds(2 * own_heads + head, 1), :] = delta

    stats[pl.ds(16, 16), :] = dot(
        stats[pl.ds(0, 16), :], pick, 1, 1, precision=lax.Precision.HIGHEST
    )
    tile_stats = stats.at[pl.ds(0, 16)]
    side_stats = stats.at[pl.ds(16, 16)]
    stat_copies = []
    for number, (src, device) in enumerate(
        (
            (tile_stats, south),
            (tile_stats, north),
            (side_stats, west),
            (side_stats, east),
            (side_stats, corners[3]),
            (side_stats, corners[2]),
            (side_stats, corners[1]),
            (side_stats, corners[0]),
        )
    ):
        stat_copies.append(start(src, stats_in.at[number], STATS + number, device))

    grad_corner_copies = []
    for number, spot_at in ((0, EAST), (1, WEST)):
        grad_side_copies[number].wait_recv()
        for leg, (device, block) in enumerate(((south, 4), (north, 5))):
            grad_corner_copies.append(
                start(
                    dos.at[pl.ds(side + spot_at, SLAB)],
                    dos.at[pl.ds(block * TOK + spot_at, SLAB)],
                    GRADS + CORNERS + 2 * number + leg,
                    device,
                )
            )

    parts = tuple((number * own_cols, own_cols) for number in (0, 2, 1))
    core_copies = []
    x_copies = [[], [], []]
    groups = ((0, 1), (2,))
    lon_copies = [[], []]

    def share_with_core(part):
        cols = pl.ds(*parts[part])
        return start(
            grads.at[own, cols],
            grads.at[pl.ds(TOK, TOK), cols],
            CORE_GRAD + part,
            other_core,
        )

    def input_terms(owner, numbers):
        rows = pl.ds(pl.multiple_of(owner * own_cols, own_cols), own_cols)
        total = None
        for number in numbers:
            term = dot(
                grads[own, pl.ds(number * own_cols, own_cols)], wbuf[number, rows, :], 1, 1
            )
            total = term if total is None else total + term
        return total

    def send_x(part):
        core_copies[part].wait_recv()
        cols = pl.ds(*parts[part])

        def terms(owner):
            rows = pl.ds(pl.multiple_of(owner * TOK, TOK), TOK)
            return dot(xt[rows, :], grads[:, cols], 1, 0)

        for step in range(1, XS):
            gx_out[step - 1, :, cols] = terms(((x + step) % XS) * 2 + core).astype(BF16)
            x_copies[part].append(
                start(
                    gx_out.at[step - 1, :, cols],
                    gx_in.at[step - 1, :, cols],
                    SUM_X + (XS - 1) * part + step - 1,
                    on_x(step),
                )
            )
        r1[:, cols] = terms(lat)

    def send_lon(group):
        for part in groups[group]:
            cols = pl.ds(*parts[part])
            for copy in x_copies[part]:
                copy.wait_recv()
            total = r1[:, cols]
            for number in range(XS - 1):
                total = total + gx_in[number, :, cols].astype(F32)
            r1[:, cols] = total
        half = own_cols // 2
        sent_cols = pl.ds(groups[group][0] * half, len(groups[group]) * half)
        for number, step in enumerate(lon_steps):
            target = on_lon(*step)
            rows = pl.ds(pl.multiple_of(target[1] * 8, 8), 8)
            for part in groups[group]:
                first = parts[part][0]
                gl_out[number, :, pl.ds(part * half, half)] = jnp.concatenate(
                    [r1[rows, pl.ds(first, half)], r1[rows, pl.ds(first + half, half)]], axis=0
                ).astype(BF16)
            lon_copies[group].append(
                start(
                    gl_out.at[number, :, sent_cols],
                    gl_in.at[number, :, sent_cols],
                    SUM_LON + len(lon_steps) * group + number,
                    target,
                )
            )

    def arrive(group):
        for copy in reversed(lon_copies[group]):
            copy.wait_recv()

    def finish(part):
        first, count = parts[part]
        half = count // 2
        folded = pl.ds(part * half, half)
        rows = pl.ds(pl.multiple_of(lon * 8, 8), 8)
        total = jnp.concatenate(
            [r1[rows, pl.ds(first, half)], r1[rows, pl.ds(first + half, half)]], axis=0
        )
        for number in range(len(lon_steps)):
            total = total + gl_in[number, :, folded].astype(F32)
        total = total * weight_scale
        grad_weight[first // own_cols, :, pl.ds(0, half)] = total[:8]
        grad_weight[first // own_cols, :, pl.ds(half, half)] = total[8:]

    @pl.loop(0, own_heads, unroll=True)
    def _(head):
        mine = lane == head
        delta = stats[pl.ds(2 * own_heads + head, 1), :]
        grad_score = (scale * (probs[head] * (own_grad_probs[head] - delta))).astype(BF16)
        acc[0] = jnp.where(mine, dot(grad_score, qkv[1], 0, 0), acc[0])

    weight_scale = 1.0 / math.sqrt(TOK * LATS * LONS)
    grads[own, pl.ds(0, own_cols)] = acc[0].astype(BF16)
    core_copies.append(share_with_core(0))

    for step in range(FSDP):
        gi_own[step] = input_terms((fsdp + step) % FSDP, (0,))
    send_x(0)
    for copy in grad_tile_copies + grad_corner_copies:
        copy.wait_recv()

    @pl.loop(0, own_heads, unroll=True)
    def _(head):
        mine = lane == head
        key = jnp.where(mine, qkv[1, own, :], 0).astype(BF16)
        value = jnp.where(mine, qkv[2, own, :], 0).astype(BF16)
        scores_in[head] = dot(key, qkv[0], 1, 1) * scale + bias_b[...]
        grad_probs[head] = dot(value, dos[...], 1, 1)

    for copy in stat_copies:
        copy.wait_recv()
    half_lane = lax.broadcasted_iota(jnp.int32, (16, TOK), 1) < 64
    stat_rows[:, pl.ds(0, TOK)] = stats[pl.ds(0, 16), :]
    stat_rows[:, pl.ds(TOK, TOK)] = stats_in[0]
    stat_rows[:, pl.ds(2 * TOK, TOK)] = stats_in[1]
    for block in range(3):
        first = 2 + 2 * block
        stat_rows[:, pl.ds((3 + block) * TOK, TOK)] = jnp.where(
            half_lane, stats_in[first], stats_in[first + 1]
        )

    @pl.loop(0, own_heads, unroll=True)
    def _(head):
        mine = lane == head
        row_max = stat_rows[pl.ds(head, 1), :]
        inv_sum = stat_rows[pl.ds(own_heads + head, 1), :]
        prob = jnp.exp(jnp.minimum(scores_in[head] - row_max, 0.0)) * inv_sum
        scores_in[head] = prob
        acc[2] = jnp.where(mine, dot(prob.astype(BF16), dos[...], 1, 0), acc[2])

    grads[own, pl.ds(2 * own_cols, own_cols)] = acc[2].astype(BF16)
    core_copies.append(share_with_core(1))

    @pl.loop(0, own_heads, unroll=True)
    def _(head):
        mine = lane == head
        delta = stat_rows[pl.ds(2 * own_heads + head, 1), :]
        grad_score = (scale * (scores_in[head] * (grad_probs[head] - delta))).astype(BF16)
        acc[1] = jnp.where(mine, dot(grad_score, qkv[0], 1, 0), acc[1])

    grads[own, pl.ds(own_cols, own_cols)] = acc[1].astype(BF16)
    core_copies.append(share_with_core(2))
    send_x(1)
    for step in range(FSDP):
        gi_own[step] = gi_own[step] + input_terms((fsdp + step) % FSDP, (2,))
    send_x(2)
    input_copies = []
    for step in range(1, FSDP):
        peer = (fsdp + step) % FSDP
        gi_out[step - 1] = (gi_own[step] + input_terms(peer, (1,))).astype(BF16)
        input_copies.append(
            start(gi_out.at[step - 1], gi_in.at[step - 1], INPUT_SUMS + step - 1, at(d_fsdp=peer))
        )
    gi_own[0] = gi_own[0] + input_terms(fsdp, (1,))
    send_lon(0)
    send_lon(1)
    for copy in input_copies:
        copy.wait_recv()
    grad_input[...] = (
        gi_own[0] + gi_in[0].astype(F32) + gi_in[1].astype(F32) + gi_in[2].astype(F32)
    ).astype(BF16)
    arrive(0)
    finish(0)
    finish(1)
    arrive(1)
    finish(2)

    for copy in sent:
        copy.wait_send()


def shards(tokens, grad_out, weight):
    rows, cols, width = tokens.shape
    own_cols = grad_out.shape[2]
    three = weight.shape[0]
    anywhere = pl.BlockSpec(memory_space=pl.ANY)
    in_vmem = pl.BlockSpec(memory_space=pltpu.VMEM)
    total = three * own_cols
    grad_input, grad_weight = pl.pallas_call(
        kernel,
        out_shape=(
            jax.ShapeDtypeStruct((TOK, own_cols), BF16),
            jax.ShapeDtypeStruct((three, 8, own_cols), F32),
        ),
        in_specs=[anywhere] * 3,
        out_specs=(in_vmem, in_vmem),
        scratch_shapes=[
            pltpu.VMEM((EXT, width), BF16),
            pltpu.VMEM((EXT, own_cols), BF16),
            pltpu.VMEM((TOK, width + own_cols), BF16),
            pltpu.VMEM((three, width, own_cols), BF16),
            pltpu.VMEM((three, EXT, own_cols), BF16),
            pltpu.VMEM((EXT, TOK), F32),
            pltpu.VMEM((TOK, EXT), F32),
            pltpu.VMEM((32, TOK), F32),
            pltpu.VMEM((8, 16, TOK), F32),
            pltpu.VMEM((16, EXT), F32),
            pltpu.VMEM((2 * TOK, total), BF16),
            pltpu.VMEM((width, 2 * TOK), BF16),
            pltpu.VMEM((own_cols // 64, EXT, TOK), F32),
            pltpu.VMEM((own_cols // 64, EXT, TOK), F32),
            pltpu.VMEM((own_cols // 64, TOK, EXT), F32),
            pltpu.VMEM((own_cols // 64, TOK, EXT), F32),
            pltpu.VMEM((three, TOK, own_cols), F32),
            pltpu.VMEM((FSDP, TOK, own_cols), F32),
            pltpu.VMEM((FSDP - 1, TOK, own_cols), BF16),
            pltpu.VMEM((FSDP - 1, TOK, own_cols), BF16),
            pltpu.VMEM((XS - 1, TOK, total), BF16),
            pltpu.VMEM((XS - 1, TOK, total), BF16),
            pltpu.VMEM((TOK, total), F32),
            pltpu.VMEM((LONS - 1, 16, total // 2), BF16),
            pltpu.VMEM((LONS - 1, 16, total // 2), BF16),
            pltpu.SemaphoreType.DMA((COPIES,)),
            pltpu.SemaphoreType.DMA((COPIES,)),
            pltpu.SemaphoreType.DMA((3,)),
        ],
        compiler_params=pltpu.CompilerParams(
            collective_id=0, has_side_effects=True, vmem_limit_bytes=63 * 1024 * 1024
        ),
    )(tokens.reshape(TOK, width), grad_out.reshape(TOK, own_cols), weight)
    return grad_input.reshape(rows, cols, own_cols), grad_weight


def solution(mesh):
    placed = (P("lat", "lon", None), P("lat", "lon", "fsdp"), P(None, "fsdp", None))
    return jax.shard_map(
        shards,
        mesh=mesh,
        in_specs=placed,
        out_specs=(P("lat", "lon", "fsdp"), P(None, ("lat", "lon"), "fsdp")),
        check_vma=False,
    )
```

```python
import functools
import math

import jax
import jax.numpy as jnp
from jax import lax
from jax.experimental import pallas as pl
from jax.experimental.pallas import tpu as pltpu
from jax.sharding import PartitionSpec as P

HEADS = 16
RADIUS = 6
MESH = pl.DeviceIdType.MESH
BF16 = jnp.bfloat16
F32 = jnp.float32

ROWS, COLS = 8, 16
TOK = ROWS * COLS
BLOCKS = 6
EXT = BLOCKS * TOK
SLAB = RADIUS * ROWS
EAST, WEST = 0, 64
LATS, LONS, FSDP = 8, 16, 4
XS, YS, ZS = 4, 8, 8

NORTH_SOUTH, EAST_WEST, CORNERS = 0, 2, 4
GRADS = 8
WEIGHTS, SIDE_WEIGHTS, CORE_WEIGHTS = 16, 19, 25
STATS = 31
CORE_GRAD = 39
INPUT_SUMS = 42
SUM_X, SUM_LON = 45, 54
COPIES = 69


def dot(a, b, ca, cb, precision=None):
    return lax.dot_general(
        a, b, (((ca,), (cb,)), ((), ())), preferred_element_type=F32, precision=precision
    )


def place(block, spot):
    half = spot // 64
    inner = spot % 64
    side_col = inner // ROWS + jnp.where(half == 0, COLS, -RADIUS)
    is_tile = block < 3
    row = jnp.where(is_tile, spot // COLS, inner % ROWS)
    col = jnp.where(is_tile, spot % COLS, side_col)
    kind = block % 3
    shift = jnp.where(kind == 1, -ROWS, jnp.where(kind == 2, ROWS, 0))
    real = is_tile | (inner < SLAB)
    return row + shift, col, real


def bias_of(block, spot, own, lat):
    row, col, real = place(block, spot)
    own_row, own_col = own // COLS, own % COLS
    gap_r = row - own_row
    gap_c = col - own_col
    grid_row = lat * ROWS + row
    allowed = (
        real
        & (gap_r <= RADIUS)
        & (gap_r >= -RADIUS)
        & (gap_c <= RADIUS)
        & (gap_c >= -RADIUS)
        & (grid_row >= 0)
        & (grid_row < LATS * ROWS)
    )
    return jnp.where(allowed, 0.0, -jnp.inf).astype(F32)


def kernel(
    tokens,
    grad_out,
    weight,
    grad_input,
    grad_weight,
    xs,
    dos,
    packs,
    wbuf,
    qkv,
    bias_f,
    bias_b,
    stats,
    stats_in,
    stat_rows,
    grads,
    xt,
    probs,
    own_grad_probs,
    scores_in,
    grad_probs,
    acc,
    gi_own,
    gi_out,
    gi_in,
    gx_out,
    gx_in,
    r1,
    gl_out,
    gl_in,
    send_sems,
    recv_sems,
    local_sems,
):
    lat = lax.axis_index("lat")
    lon = lax.axis_index("lon")
    fsdp = lax.axis_index("fsdp")
    x, core = lat // 2, lat % 2
    z_hi, y = lon // YS, lon % YS
    z = z_hi * FSDP + fsdp
    head_size = 64
    own_heads = HEADS // FSDP
    own_cols = own_heads * head_size
    width = FSDP * own_cols
    scale = 1.0 / math.sqrt(head_size)

    def at(*, d_lat=None, d_lon=None, d_fsdp=None):
        return (
            lat if d_lat is None else d_lat,
            lon if d_lon is None else d_lon,
            fsdp if d_fsdp is None else d_fsdp,
        )

    south_lat, north_lat = (lat + 1) % LATS, (lat + LATS - 1) % LATS
    east_lon, west_lon = (lon + 1) % LONS, (lon + LONS - 1) % LONS
    east_fsdp = jnp.where(y == YS - 1, FSDP - 1 - fsdp, fsdp)
    west_fsdp = jnp.where(y == 0, FSDP - 1 - fsdp, fsdp)
    south, north = at(d_lat=south_lat), at(d_lat=north_lat)
    east, west = at(d_lon=east_lon), at(d_lon=west_lon)
    east_copy = at(d_lon=east_lon, d_fsdp=east_fsdp)
    west_copy = at(d_lon=west_lon, d_fsdp=west_fsdp)
    other_core = at(d_lat=lat + 1 - 2 * core)

    def on_z(step):
        target = (z + step + ZS) % ZS
        return at(d_lon=(target // FSDP) * YS + y, d_fsdp=target % FSDP)

    def on_x(step):
        return at(d_lat=((x + step) % XS) * 2 + core)

    def on_y(step):
        return at(d_lon=z_hi * YS + (y + step) % YS)

    def on_lon(cross, step):
        half = 1 - z_hi if cross else z_hi
        return at(d_lon=half * YS + (y + step) % YS)

    corners = (
        at(d_lat=north_lat, d_lon=east_lon),
        at(d_lat=north_lat, d_lon=west_lon),
        at(d_lat=south_lat, d_lon=east_lon),
        at(d_lat=south_lat, d_lon=west_lon),
    )
    partners = [*corners, east_copy, west_copy, south, north]
    partners += [on_z(step) for step in (1, -1, 2, -2)]
    partners += [at(d_fsdp=(fsdp + step) % FSDP) for step in range(1, FSDP)]
    partners += [on_x(step) for step in range(1, XS)]
    lon_steps = [(1, step) for step in range(YS)] + [(0, step) for step in range(1, YS)]
    partners += [on_lon(*step) for step in lon_steps]

    barrier = pltpu.get_barrier_semaphore()
    for partner in partners:
        pl.semaphore_signal(barrier, inc=1, device_id=partner, device_id_type=MESH)

    own_tokens = pltpu.make_async_copy(tokens, xs.at[pl.ds(0, TOK)], local_sems.at[0])
    own_grads = pltpu.make_async_copy(grad_out, dos.at[pl.ds(0, TOK)], local_sems.at[1])
    own_start = pl.multiple_of(fsdp * own_cols, own_cols)
    own_weight = pltpu.make_async_copy(
        weight.at[:, :, pl.ds(own_start, own_cols)],
        wbuf.at[:, pl.ds(own_start, own_cols), :],
        local_sems.at[2],
    )
    own_tokens.start()
    own_grads.start()
    own_weight.start()

    def remote(src, dst, number, device):
        return pltpu.make_async_remote_copy(
            src_ref=src,
            dst_ref=dst,
            send_sem=send_sems.at[number],
            recv_sem=recv_sems.at[number],
            device_id=device,
            device_id_type=MESH,
        )

    pl.semaphore_wait(barrier, len(partners))

    sent = []

    def start(*args):
        copy = remote(*args)
        copy.start()
        sent.append(copy)
        return copy

    half_rows = own_cols // 2
    quarter = half_rows // 2
    eighth = quarter // 2
    parity = y % 2
    far = 2 - 4 * core
    mine_at = core * half_rows + parity * quarter
    other_at = core * half_rows + (1 - parity) * quarter

    def weight_rows(origin, offset, count):
        first = pl.multiple_of(origin * own_cols + offset, eighth)
        return wbuf.at[:, pl.ds(first, count), :]

    weight_copies = []
    for number, step in enumerate((1, -1, far)):
        target = on_z(step)
        cols = pl.multiple_of(target[2] * own_cols, own_cols)
        weight_copies.append(
            start(
                weight.at[
                    :, pl.ds(pl.multiple_of(mine_at, quarter), quarter), pl.ds(cols, own_cols)
                ],
                weight_rows(fsdp, mine_at, quarter),
                WEIGHTS + number,
                target,
            )
        )

    tile_copies = []
    for number, device, block in ((0, south, 1), (1, north, 2)):
        tile_copies.append(
            start(
                tokens, xs.at[pl.ds(block * TOK, TOK)], NORTH_SOUTH + number, device
            )
        )
    grad_tile_copies = []
    for number, device, block in ((0, south, 1), (1, north, 2)):
        grad_tile_copies.append(
            start(
                grad_out,
                dos.at[pl.ds(block * TOK, TOK)],
                GRADS + NORTH_SOUTH + number,
                device,
            )
        )

    own_tokens.wait()
    own_grads.wait()
    spot = lax.broadcasted_iota(jnp.int32, (TOK, TOK), 0)
    flat = lax.broadcasted_iota(jnp.int32, (TOK, TOK), 1)
    inner = spot % 64
    source = (inner % ROWS) * COLS + inner // ROWS + jnp.where(spot < 64, 0, COLS - RADIUS)
    picks = (inner < SLAB) & (flat == source)
    pick = jnp.where(picks, 1.0, 0.0).astype(F32)
    pick_16 = pick.astype(BF16)
    packs[:, pl.ds(0, width)] = dot(pick_16, xs[pl.ds(0, TOK), :], 1, 0).astype(BF16)
    packs[:, pl.ds(width, own_cols)] = dot(pick_16, dos[pl.ds(0, TOK), :], 1, 0).astype(BF16)
    side_copies = []
    side = 3 * TOK
    for number, spot_at, token_device in ((0, EAST, west_copy), (1, WEST, east_copy)):
        side_copies.append(
            start(
                packs.at[pl.ds(spot_at, SLAB), pl.ds(0, width)],
                xs.at[pl.ds(side + spot_at, SLAB)],
                EAST_WEST + number,
                token_device,
            )
        )
    xt[:, pl.ds(0, TOK)] = xs[pl.ds(0, TOK), :].T

    for block in range(3, BLOCKS):
        for spot_at in (EAST, WEST):
            unused = pl.ds(block * TOK + spot_at + SLAB, 64 - SLAB)
            xs[unused, :] = jnp.zeros((64 - SLAB, width), BF16)
            dos[unused, :] = jnp.zeros((64 - SLAB, own_cols), BF16)

    @pl.loop(0, BLOCKS)
    def _(block):
        first = pl.multiple_of(block * TOK, TOK)
        bias_f[pl.ds(first, TOK), :] = bias_of(block, spot, flat, lat)
        bias_b[:, pl.ds(first, TOK)] = bias_of(block, flat, spot, lat)

    side_weight_copies = []
    core_weight_copies = []
    origins = [(fsdp + step + FSDP) % FSDP for step in (-1, 1, -far)]
    for number, origin in enumerate(origins):
        weight_copies[number].wait_recv()
        for leg, step in enumerate((1, -1)):
            region = weight_rows(origin, mine_at + leg * eighth, eighth)
            side_weight_copies.append(
                start(region, region, SIDE_WEIGHTS + 2 * number + leg, on_y(step))
            )
        region = weight_rows(origin, mine_at, quarter)
        core_weight_copies.append(start(region, region, CORE_WEIGHTS + 2 * number, other_core))
    corner_copies = []
    for number, spot_at in ((0, EAST), (1, WEST)):
        side_copies[number].wait_recv()
        for leg, (device, block) in enumerate(((south, 4), (north, 5))):
            corner_copies.append(
                start(
                    xs.at[pl.ds(side + spot_at, SLAB)],
                    xs.at[pl.ds(block * TOK + spot_at, SLAB)],
                    CORNERS + 2 * number + leg,
                    device,
                )
            )
    grad_side_copies = []
    for number, spot_at, device in ((0, EAST, west), (1, WEST, east)):
        grad_side_copies.append(
            start(
                packs.at[pl.ds(spot_at, SLAB), pl.ds(width, own_cols)],
                dos.at[pl.ds(side + spot_at, SLAB)],
                GRADS + EAST_WEST + number,
                device,
            )
        )

    for copy in tile_copies:
        copy.wait_recv()
    pair_rows = pl.ds(pl.multiple_of((2 - core) * TOK, TOK), TOK)
    xt[:, pl.ds(TOK, TOK)] = xs[pair_rows, :].T
    for number, origin in enumerate(origins):
        for leg in range(2):
            side_weight_copies[2 * number + leg].wait_recv()
        region = weight_rows(origin, other_at, quarter)
        core_weight_copies.append(start(region, region, CORE_WEIGHTS + 2 * number + 1, other_core))
    own_weight.wait()
    for copy in core_weight_copies + corner_copies:
        copy.wait_recv()

    @pl.loop(0, EXT // 256)
    def _(step):
        rows = pl.ds(pl.multiple_of(step * 256, 256), 256)
        block = xs[rows, :]
        for number in range(3):
            qkv[number, rows, :] = dot(block, wbuf[number], 1, 0).astype(BF16)

    lane = lax.broadcasted_iota(jnp.int32, (TOK, own_cols), 1) // head_size
    own = pl.ds(0, TOK)

    stats[pl.ds(3 * own_heads, own_heads), :] = jnp.zeros((own_heads, TOK), F32)

    @pl.loop(0, own_heads, unroll=True)
    def _(head):
        mine = lane == head
        query = jnp.where(mine, qkv[0, own, :], 0).astype(BF16)
        cotangent = jnp.where(mine, dos[own, :], 0).astype(BF16)
        scores = dot(qkv[1], query, 1, 1) * scale + bias_f[...]
        row_max = jnp.max(scores, axis=0, keepdims=True)
        prob = jnp.exp(scores - row_max)
        inv_sum = 1.0 / jnp.sum(prob, axis=0, keepdims=True)
        prob = prob * inv_sum
        grad_prob = dot(qkv[2], cotangent, 1, 1)
        delta = jnp.sum(prob * grad_prob, axis=0, keepdims=True)
        probs[head] = prob
        own_grad_probs[head] = grad_prob
        stats[pl.ds(head, 1), :] = row_max
        stats[pl.ds(own_heads + head, 1), :] = inv_sum
        stats[pl.ds(2 * own_heads + head, 1), :] = delta

    stats[pl.ds(16, 16), :] = dot(
        stats[pl.ds(0, 16), :], pick, 1, 1, precision=lax.Precision.HIGHEST
    )
    tile_stats = stats.at[pl.ds(0, 16)]
    side_stats = stats.at[pl.ds(16, 16)]
    stat_copies = []
    for number, (src, device) in enumerate(
        (
            (tile_stats, south),
            (tile_stats, north),
            (side_stats, west),
            (side_stats, east),
            (side_stats, corners[3]),
            (side_stats, corners[2]),
            (side_stats, corners[1]),
            (side_stats, corners[0]),
        )
    ):
        stat_copies.append(start(src, stats_in.at[number], STATS + number, device))

    grad_corner_copies = []
    for number, spot_at in ((0, EAST), (1, WEST)):
        grad_side_copies[number].wait_recv()
        for leg, (device, block) in enumerate(((south, 4), (north, 5))):
            grad_corner_copies.append(
                start(
                    dos.at[pl.ds(side + spot_at, SLAB)],
                    dos.at[pl.ds(block * TOK + spot_at, SLAB)],
                    GRADS + CORNERS + 2 * number + leg,
                    device,
                )
            )

    parts = tuple((number * own_cols, own_cols) for number in (0, 2, 1))
    core_copies = []
    x_copies = [[], [], []]
    groups = ((0, 1, 2),)
    lon_copies = [[]]

    def share_with_core(part):
        cols = pl.ds(*parts[part])
        return start(
            grads.at[own, cols],
            grads.at[pl.ds(TOK, TOK), cols],
            CORE_GRAD + part,
            other_core,
        )

    def input_terms(owner, numbers):
        rows = pl.ds(pl.multiple_of(owner * own_cols, own_cols), own_cols)
        total = None
        for number in numbers:
            term = dot(
                grads[own, pl.ds(number * own_cols, own_cols)], wbuf[number, rows, :], 1, 1
            )
            total = term if total is None else total + term
        return total

    def send_x(part):
        core_copies[part].wait_recv()
        cols = pl.ds(*parts[part])

        def terms(owner):
            rows = pl.ds(pl.multiple_of(owner * TOK, TOK), TOK)
            return dot(xt[rows, :], grads[:, cols], 1, 0)

        for step in range(1, XS):
            gx_out[step - 1, :, cols] = terms(((x + step) % XS) * 2 + core).astype(BF16)
            x_copies[part].append(
                start(
                    gx_out.at[step - 1, :, cols],
                    gx_in.at[step - 1, :, cols],
                    SUM_X + (XS - 1) * part + step - 1,
                    on_x(step),
                )
            )
        r1[:, cols] = terms(lat)

    def send_lon(group):
        for part in groups[group]:
            cols = pl.ds(*parts[part])
            for copy in x_copies[part]:
                copy.wait_recv()
            total = r1[:, cols]
            for number in range(XS - 1):
                total = total + gx_in[number, :, cols].astype(F32)
            r1[:, cols] = total
        half = own_cols // 2
        sent_cols = pl.ds(groups[group][0] * half, len(groups[group]) * half)
        for number, step in enumerate(lon_steps):
            target = on_lon(*step)
            rows = pl.ds(pl.multiple_of(target[1] * 8, 8), 8)
            for part in groups[group]:
                first = parts[part][0]
                gl_out[number, :, pl.ds(part * half, half)] = jnp.concatenate(
                    [r1[rows, pl.ds(first, half)], r1[rows, pl.ds(first + half, half)]], axis=0
                ).astype(BF16)
            lon_copies[group].append(
                start(
                    gl_out.at[number, :, sent_cols],
                    gl_in.at[number, :, sent_cols],
                    SUM_LON + len(lon_steps) * group + number,
                    target,
                )
            )

    def arrive(group):
        for copy in reversed(lon_copies[group]):
            copy.wait_recv()

    def finish(part):
        first, count = parts[part]
        half = count // 2
        folded = pl.ds(part * half, half)
        rows = pl.ds(pl.multiple_of(lon * 8, 8), 8)
        total = jnp.concatenate(
            [r1[rows, pl.ds(first, half)], r1[rows, pl.ds(first + half, half)]], axis=0
        )
        for number in range(len(lon_steps)):
            total = total + gl_in[number, :, folded].astype(F32)
        total = total * weight_scale
        grad_weight[first // own_cols, :, pl.ds(0, half)] = total[:8]
        grad_weight[first // own_cols, :, pl.ds(half, half)] = total[8:]

    @pl.loop(0, own_heads, unroll=True)
    def _(head):
        mine = lane == head
        delta = stats[pl.ds(2 * own_heads + head, 1), :]
        grad_score = (scale * (probs[head] * (own_grad_probs[head] - delta))).astype(BF16)
        acc[0] = jnp.where(mine, dot(grad_score, qkv[1], 0, 0), acc[0])

    weight_scale = 1.0 / math.sqrt(TOK * LATS * LONS)
    grads[own, pl.ds(0, own_cols)] = acc[0].astype(BF16)
    core_copies.append(share_with_core(0))

    for step in range(FSDP):
        gi_own[step] = input_terms((fsdp + step) % FSDP, (0,))
    send_x(0)
    for copy in grad_tile_copies + grad_corner_copies:
        copy.wait_recv()

    @pl.loop(0, own_heads, unroll=True)
    def _(head):
        mine = lane == head
        key = jnp.where(mine, qkv[1, own, :], 0).astype(BF16)
        value = jnp.where(mine, qkv[2, own, :], 0).astype(BF16)
        scores_in[head] = dot(key, qkv[0], 1, 1) * scale + bias_b[...]
        grad_probs[head] = dot(value, dos[...], 1, 1)

    for copy in stat_copies:
        copy.wait_recv()
    half_lane = lax.broadcasted_iota(jnp.int32, (16, TOK), 1) < 64
    stat_rows[:, pl.ds(0, TOK)] = stats[pl.ds(0, 16), :]
    stat_rows[:, pl.ds(TOK, TOK)] = stats_in[0]
    stat_rows[:, pl.ds(2 * TOK, TOK)] = stats_in[1]
    for block in range(3):
        first = 2 + 2 * block
        stat_rows[:, pl.ds((3 + block) * TOK, TOK)] = jnp.where(
            half_lane, stats_in[first], stats_in[first + 1]
        )

    @pl.loop(0, own_heads, unroll=True)
    def _(head):
        mine = lane == head
        row_max = stat_rows[pl.ds(head, 1), :]
        inv_sum = stat_rows[pl.ds(own_heads + head, 1), :]
        prob = jnp.exp(jnp.minimum(scores_in[head] - row_max, 0.0)) * inv_sum
        scores_in[head] = prob
        acc[2] = jnp.where(mine, dot(prob.astype(BF16), dos[...], 1, 0), acc[2])

    grads[own, pl.ds(2 * own_cols, own_cols)] = acc[2].astype(BF16)
    core_copies.append(share_with_core(1))

    @pl.loop(0, own_heads, unroll=True)
    def _(head):
        mine = lane == head
        delta = stat_rows[pl.ds(2 * own_heads + head, 1), :]
        grad_score = (scale * (scores_in[head] * (grad_probs[head] - delta))).astype(BF16)
        acc[1] = jnp.where(mine, dot(grad_score, qkv[0], 1, 0), acc[1])

    grads[own, pl.ds(own_cols, own_cols)] = acc[1].astype(BF16)
    core_copies.append(share_with_core(2))
    send_x(1)
    for step in range(FSDP):
        gi_own[step] = gi_own[step] + input_terms((fsdp + step) % FSDP, (2,))
    send_x(2)
    input_copies = []
    for step in range(1, FSDP):
        peer = (fsdp + step) % FSDP
        gi_out[step - 1] = (gi_own[step] + input_terms(peer, (1,))).astype(BF16)
        input_copies.append(
            start(gi_out.at[step - 1], gi_in.at[step - 1], INPUT_SUMS + step - 1, at(d_fsdp=peer))
        )
    gi_own[0] = gi_own[0] + input_terms(fsdp, (1,))
    send_lon(0)
    for copy in input_copies:
        copy.wait_recv()
    grad_input[...] = (
        gi_own[0] + gi_in[0].astype(F32) + gi_in[1].astype(F32) + gi_in[2].astype(F32)
    ).astype(BF16)
    arrive(0)
    finish(0)
    finish(1)
    finish(2)

    for copy in sent:
        copy.wait_send()


def shards(tokens, grad_out, weight):
    rows, cols, width = tokens.shape
    own_cols = grad_out.shape[2]
    three = weight.shape[0]
    anywhere = pl.BlockSpec(memory_space=pl.ANY)
    in_vmem = pl.BlockSpec(memory_space=pltpu.VMEM)
    total = three * own_cols
    grad_input, grad_weight = pl.pallas_call(
        kernel,
        out_shape=(
            jax.ShapeDtypeStruct((TOK, own_cols), BF16),
            jax.ShapeDtypeStruct((three, 8, own_cols), F32),
        ),
        in_specs=[anywhere] * 3,
        out_specs=(in_vmem, in_vmem),
        scratch_shapes=[
            pltpu.VMEM((EXT, width), BF16),
            pltpu.VMEM((EXT, own_cols), BF16),
            pltpu.VMEM((TOK, width + own_cols), BF16),
            pltpu.VMEM((three, width, own_cols), BF16),
            pltpu.VMEM((three, EXT, own_cols), BF16),
            pltpu.VMEM((EXT, TOK), F32),
            pltpu.VMEM((TOK, EXT), F32),
            pltpu.VMEM((32, TOK), F32),
            pltpu.VMEM((8, 16, TOK), F32),
            pltpu.VMEM((16, EXT), F32),
            pltpu.VMEM((2 * TOK, total), BF16),
            pltpu.VMEM((width, 2 * TOK), BF16),
            pltpu.VMEM((own_cols // 64, EXT, TOK), F32),
            pltpu.VMEM((own_cols // 64, EXT, TOK), F32),
            pltpu.VMEM((own_cols // 64, TOK, EXT), F32),
            pltpu.VMEM((own_cols // 64, TOK, EXT), F32),
            pltpu.VMEM((three, TOK, own_cols), F32),
            pltpu.VMEM((FSDP, TOK, own_cols), F32),
            pltpu.VMEM((FSDP - 1, TOK, own_cols), BF16),
            pltpu.VMEM((FSDP - 1, TOK, own_cols), BF16),
            pltpu.VMEM((XS - 1, TOK, total), BF16),
            pltpu.VMEM((XS - 1, TOK, total), BF16),
            pltpu.VMEM((TOK, total), F32),
            pltpu.VMEM((LONS - 1, 16, total // 2), BF16),
            pltpu.VMEM((LONS - 1, 16, total // 2), BF16),
            pltpu.SemaphoreType.DMA((COPIES,)),
            pltpu.SemaphoreType.DMA((COPIES,)),
            pltpu.SemaphoreType.DMA((3,)),
        ],
        compiler_params=pltpu.CompilerParams(
            collective_id=0, has_side_effects=True, vmem_limit_bytes=63 * 1024 * 1024
        ),
    )(tokens.reshape(TOK, width), grad_out.reshape(TOK, own_cols), weight)
    return grad_input.reshape(rows, cols, own_cols), grad_weight


def solution(mesh):
    placed = (P("lat", "lon", None), P("lat", "lon", "fsdp"), P(None, "fsdp", None))
    return jax.shard_map(
        shards,
        mesh=mesh,
        in_specs=placed,
        out_specs=(P("lat", "lon", "fsdp"), P(None, ("lat", "lon"), "fsdp")),
        check_vma=False,
    )
```
